128 devices in a mesh: row: 8 (over y_hi, z), col: 16 (over x, y_lo, core).
Axes of the slice: x: 4, y: 4 (y_hi: 2, y_lo: 2; y = y_hi * 2 + y_lo), z: 4, core: 2. Of those that a mesh axis runs over, the one named last changes fastest.
Arguments:
- tokens: bfloat16 [6144, 8192], P('row', 'col'), may hold values from -6 to 6
- gate_weight: bfloat16 [8192, 14336], P('row', 'col'), may hold values from -0.0625 to 0.0625
- up_weight: bfloat16 [8192, 14336], P('row', 'col'), may hold values from -0.0625 to 0.0625
Outputs:
- hidden: bfloat16 [6144, 14336], P('row', 'col')
The draws below stay inside these ranges and needn't reach their ends.
All inputs are finite; a program needn't handle non-finite values.
Results may differ from the reference program's by a relative error of at most 0.0023.
Values may be sent and summed in bfloat16 or wider, within the bound.
A program may use at most 192 MiB of HBM per device.

```python
import jax
import jax.numpy as jnp

D = 8192
FF_WIN = 14336
TOKENS = 6144


def block_levels(rng, extent, cuts, least, largest):
    gain = 1.0
    for position, parts in cuts:
        steps = jax.random.uniform(jax.random.fold_in(jax.random.fold_in(rng, 6), position), (parts,), jnp.float32, least / len(cuts), largest / len(cuts))
        gain = gain * jnp.repeat(jnp.exp(steps), extent[position] // parts).reshape((-1,) + (1,) * (len(extent) - 1 - position))
    return gain


def scatter_about(key, shape, spread, limit, split=(), held_as=jnp.bfloat16):
    entries = spread * jax.random.normal(key, shape, jnp.float32)
    if split:
        entries = entries * block_levels(key, shape, split, -0.22, 0.18)
    return jnp.clip(entries, -limit, limit).astype(held_as)


def setup_inputs(seed: int = 0) -> dict:
    seeds = jax.random.split(jax.random.key(seed), 4)
    tokens = scatter_about(seeds[0], (TOKENS, D), 1.0, 6.0, ((0, 8), (1, 16)))
    gate_weight = scatter_about(seeds[1], (D, FF_WIN), D ** -0.5, 0.0625, ((0, 8), (1, 16)))
    up_weight = scatter_about(seeds[2], (D, FF_WIN), D ** -0.5, 0.0625, ((0, 8), (1, 16)))
    return dict(tokens=tokens, gate_weight=gate_weight, up_weight=up_weight)


def reference(tokens, gate_weight, up_weight):
    gate = jnp.dot(tokens, gate_weight, preferred_element_type=jnp.float32)
    up = jnp.dot(tokens, up_weight, preferred_element_type=jnp.float32)
    return (jax.nn.silu(gate) * up).astype(jnp.bfloat16)
```

```python
import functools

import jax
import jax.numpy as jnp
from jax import lax
from jax.experimental import pallas as pl
from jax.experimental.pallas import tpu as pltpu
from jax.sharding import PartitionSpec as P

MESH = pl.DeviceIdType.MESH
LANES = 128
PIECES = 3


def encode(v):
    w = v * 2.0**14
    w2 = w * w
    return (w2 * w2 * w).astype(jnp.bfloat16)


def decode(u):
    u = u.astype(jnp.float32)
    r = jnp.exp2(jnp.log2(jnp.abs(u)) * 0.2 - 14.0)
    return jnp.where(u < 0, -r, r)


def kernel(
    tok, gate, up, out,
    wb, tb, send, got, acc,
    w_in, w_out, w_local, t_in, t_sib, y_out, x_out, s_out, o_in, o_out,
):
    rows, half = tok.shape
    depth, units = gate.shape
    chunks = units // LANES
    piece = rows // PIECES
    row, col = lax.axis_index("row"), lax.axis_index("col")
    yh, z = row // 4, row % 4
    x, yl, core = col // 4, (col // 2) % 2, col % 2
    b = x % 2
    source = (x // 2) == yh
    y = yh * 2 + yl

    def at(x=x, y=y, z=z, core=core):
        return ((y // 2) * 4 + z, x * 4 + (y % 2) * 2 + core)

    z_next, z_prev = (z + 1) % 4, (z + 3) % 4
    x_next, x_prev = (x + 1) % 4, (x + 3) % 4
    right, left = at(z=z_next), at(z=z_prev)
    partner = at(y=(y + 2) % 4)
    flip = at(y=yh * 2 + 1 - yl)
    cross = at(y=(1 - yh) * 2 + 1 - yl)
    sibling = at(core=1 - core)
    pair = at(x=jnp.where(b == 0, x_next, x_prev))
    outer = at(x=jnp.where(b == 0, x_prev, x_next))

    def remote(src, dst, ssem, rsem, to):
        return pltpu.make_async_remote_copy(
            src_ref=src, dst_ref=dst, send_sem=ssem, recv_sem=rsem, device_id=to, device_id_type=MESH
        )

    def landed(ref, sem):
        pltpu.make_async_copy(ref, ref, sem).wait()

    def slot(n, s, lo=0, size=depth):
        return wb.at[n, pl.ds(pl.multiple_of(s * depth + lo, size), size), :]

    def pack(n):
        mine = pl.ds(pl.multiple_of(z * depth, depth), depth)
        lane = pl.ds(pl.multiple_of(n * LANES, LANES), LANES)
        return (
            pltpu.make_async_copy(gate.at[:, lane], wb.at[n, mine, pl.ds(0, LANES)], w_local.at[n, 0]),
            pltpu.make_async_copy(up.at[:, lane], wb.at[n, mine, pl.ds(LANES, LANES)], w_local.at[n, 1]),
        )

    def own_weights(n):
        mine = slot(n, z)
        return (
            remote(mine, mine, w_out.at[n, 0], w_in.at[n, 0], right),
            remote(mine, mine, w_out.at[n, 1], w_in.at[n, 1], left),
        )

    def relayed_weights(n):
        top = slot(n, z_prev, 0, depth // 2)
        low = slot(n, z_next, depth // 2, depth // 2)
        return (
            remote(top, top, w_out.at[n, 2], w_in.at[n, 2], right),
            remote(low, low, w_out.at[n, 3], w_in.at[n, 3], left),
        )

    def start_own(n):
        for copy in pack(n):
            copy.wait()
        for copy in own_weights(n):
            copy.start()

    def weights_step(n, ahead=True):
        first, second = relayed_weights(n)
        landed(slot(n, z_prev), w_in.at[n, 0])
        first.start()
        landed(slot(n, z_next), w_in.at[n, 1])
        second.start()
        if ahead:
            @pl.when(n + 2 < chunks)
            def _():
                start_own(n + 2)

    def weights_ready(n):
        far = (z + 2) % 4
        landed(slot(n, far, 0, depth // 2), w_in.at[n, 2])
        landed(slot(n, far, depth // 2, depth // 2), w_in.at[n, 3])

    def block(r, p, j, c):
        return tb.at[
            r,
            pl.ds(pl.multiple_of(p * piece, piece), piece),
            pl.ds(pl.multiple_of(j * 2 * half + c * half, half), half),
        ]

    own_j = b * 2 + yl

    def token_sends(p):
        mine = tok.at[pl.ds(p * piece, piece), :]
        near = [remote(mine, block(1, p, own_j, core), y_out.at[0, p], t_in.at[1, p, own_j], flip)]
        far = [
            remote(mine, block(0, p, own_j, core), y_out.at[0, p], t_in.at[0, p, own_j], cross),
            remote(mine, block(0, p, own_j, core), y_out.at[1, p], t_in.at[0, p, own_j], partner),
        ]
        kept = pltpu.make_async_copy(mine, block(1, p, own_j, core), t_in.at[1, p, own_j])
        return near, far, kept

    def split(i):
        return i // (2 * PIECES), (i % (2 * PIECES)) // 2, i % 2

    def to_sibling(r, p, j, i, g):
        here = block(r, p, j, core)
        return remote(here, here, s_out.at[i, g], t_sib.at[r, p, j], sibling)

    def outward(r, p, j, i, e, to):
        here = block(r, p, j, core)
        return remote(here, here, x_out.at[i, e], t_in.at[r, p, j], to)

    steps = 4 * PIECES

    def near_step(i):
        r, p, q = split(i)
        j = b * 2 + q

        @pl.when(source)
        def _():
            landed(block(r, p, j, core), t_in.at[r, p, j])
            outward(r, p, j, i, 0, pair).start()
            outward(r, p, j, i, 1, outer).start()
            to_sibling(r, p, j, i, 0).start()

    def far_step(i):
        r, p, q = split(i)
        j = (1 - b) * 2 + q
        landed(block(r, p, j, core), t_in.at[r, p, j])

        @pl.when(jnp.logical_not(source))
        def _():
            outward(r, p, j, i, 0, pair).start()

        to_sibling(r, p, j, i, 1).start()

    def last_step(i):
        r, p, q = split(i)
        j = b * 2 + q

        @pl.when(jnp.logical_not(source))
        def _():
            landed(block(r, p, j, core), t_in.at[r, p, j])
            to_sibling(r, p, j, i, 0).start()

    def token_step(i):
        @pl.when(i < steps)
        def _():
            near_step(i)

        @pl.when(jnp.logical_and(i >= 2, i < steps + 2))
        def _():
            far_step(i - 2)

        @pl.when(jnp.logical_and(i >= 3, i < steps + 3))
        def _():
            last_step(i - 3)

    def tokens_ready(r):
        @pl.loop(0, PIECES * 4)
        def _(i):
            p, j = i // 4, i % 4
            landed(block(r, p, j, 1 - core), t_sib.at[r, p, j])

    def product(r, m, n):
        return jnp.dot(
            tb[r, pl.ds(pl.multiple_of(m * piece, piece), piece), :], wb[n], preferred_element_type=jnp.float32
        )

    def partial(n):
        return remote(send.at[n], got.at[n], o_out.at[n], o_in.at[n], partner)

    def send_part(n):
        @pl.loop(0, PIECES)
        def _(m):
            send[n, pl.ds(pl.multiple_of(m * piece, piece), piece), :] = encode(product(0, m, n))

        partial(n).start()

    def own_part(n):
        @pl.loop(0, PIECES)
        def _(m):
            acc[pl.ds(pl.multiple_of(m * piece, piece), piece), :] = product(1, m, n)

        landed(got.at[n], o_in.at[n])

        @pl.loop(0, rows // 32)
        def _(m):
            here = pl.ds(pl.multiple_of(m * 32, 32), 32)
            total = acc[here, :] + decode(got[n, here, :])
            g, u = total[:, :LANES], total[:, LANES:]
            out[here, pl.ds(pl.multiple_of(n * LANES, LANES), LANES)] = (g / (1.0 + jnp.exp(-g)) * u).astype(out.dtype)

    for n in range(chunks):
        for copy in pack(n):
            copy.start()

    barrier = pltpu.get_barrier_semaphore()
    neighbours = (right, left, partner, flip, cross, sibling, pair, outer)
    for to in neighbours:
        pl.semaphore_signal(barrier, inc=1, device_id=to, device_id_type=MESH)
    pl.semaphore_wait(barrier, len(neighbours))

    start_own(0)
    for p in range(PIECES):
        near, far, kept = token_sends(p)

        @pl.when(source)
        def _():
            for copy in near:
                copy.start()
            kept.start()

        @pl.when(jnp.logical_not(source))
        def _():
            for copy in far:
                copy.start()

    start_own(1)

    token_step(jnp.int32(0))
    weights_step(0)
    for i in (1, 2):
        token_step(jnp.int32(i))
    weights_step(1)
    for i in (3, 4, 5):
        token_step(jnp.int32(i))
    weights_step(2)
    for i in (6, 7, 8):
        token_step(jnp.int32(i))
    tokens_ready(0)

    @pl.loop(0, chunks + 1)
    def _(i):
        @pl.when(jnp.logical_and(i >= 2, i + 1 < chunks))
        def _():
            weights_step(i + 1)

        @pl.loop(jnp.where(i == 0, 9, jnp.clip(6 + 3 * i, 9, steps + 3)), jnp.where(i == 0, 9, jnp.clip(9 + 3 * i, 9, steps + 3)))
        def _(s):
            token_step(s)

        @pl.when(i == 3)
        def _():
            tokens_ready(1)

        @pl.when(i < chunks)
        def _():
            weights_ready(i)
            send_part(i)

        @pl.loop(jnp.where(i <= 3, 0, i - 1), jnp.where(i < 3, 0, jnp.where(i == 3, 3, i)))
        def _(n):
            own_part(n)

    @pl.loop(0, chunks)
    def _(n):
        for copy in own_weights(n) + relayed_weights(n):
            copy.wait_send()
        partial(n).wait_send()

    for p in range(PIECES):
        near, far, _ = token_sends(p)

        @pl.when(source)
        def _():
            for copy in near:
                copy.wait_send()

        @pl.when(jnp.logical_not(source))
        def _():
            for copy in far:
                copy.wait_send()

    @pl.loop(0, steps)
    def _(i):
        r, p, q = split(i)
        j = b * 2 + q
        outward(r, p, j, i, 0, pair).wait_send()
        to_sibling(r, p, j, i, 0).wait_send()
        to_sibling(r, p, j, i, 1).wait_send()

        @pl.when(source)
        def _():
            outward(r, p, j, i, 1, outer).wait_send()


def on_device(tokens, gate_weight, up_weight):
    rows, half = tokens.shape
    depth, units = gate_weight.shape
    chunks = units // LANES
    dma = pltpu.SemaphoreType.DMA
    return pl.pallas_call(
        kernel,
        out_shape=jax.ShapeDtypeStruct((rows, units), jnp.bfloat16),
        in_specs=[pl.BlockSpec(memory_space=pl.ANY)] * 3,
        out_specs=pl.BlockSpec(memory_space=pltpu.VMEM),
        scratch_shapes=[
            pltpu.VMEM((chunks, 4 * depth, 2 * LANES), jnp.bfloat16),
            pltpu.VMEM((2, rows, 8 * half), jnp.bfloat16),
            pltpu.VMEM((chunks, rows, 2 * LANES), jnp.bfloat16),
            pltpu.VMEM((chunks, rows, 2 * LANES), jnp.bfloat16),
            pltpu.VMEM((rows, 2 * LANES), jnp.float32),
            dma((chunks, 4)),
            dma((chunks, 4)),
            dma((chunks, 2)),
            dma((2, PIECES, 4)),
            dma((2, PIECES, 4)),
            dma((2, PIECES)),
            dma((4 * PIECES, 2)),
            dma((4 * PIECES, 2)),
            dma((chunks,)),
            dma((chunks,)),
        ],
        compiler_params=pltpu.CompilerParams(
            collective_id=0, has_side_effects=True, vmem_limit_bytes=60 * 2**20
        ),
        cost_estimate=pl.CostEstimate(
            flops=2 * rows * 16 * half * units * 2, bytes_accessed=2 * (rows * half + 2 * depth * units + rows * units), transcendentals=0
        ),
    )(tokens, gate_weight, up_weight)


def solution(mesh):
    placed = (P("row", "col"), P("row", "col"), P("row", "col"))
    return jax.shard_map(
        on_device, mesh=mesh, in_specs=placed, out_specs=P("row", "col"), check_vma=False
    )
```

```python
import functools

import jax
import jax.numpy as jnp
from jax import lax
from jax.experimental import pallas as pl
from jax.experimental.pallas import tpu as pltpu
from jax.sharding import PartitionSpec as P

MESH = pl.DeviceIdType.MESH
LANES = 128
PIECES = 3


def encode(v):
    w = v * 2.0**14
    w2 = w * w
    return (w2 * w2 * w).astype(jnp.bfloat16)


def decode(u):
    u = u.astype(jnp.float32)
    r = jnp.exp2(jnp.log2(jnp.abs(u)) * 0.2 - 14.0)
    return jnp.where(u < 0, -r, r)


def kernel(
    tok, gate, up, out,
    wb, tb, send, got, acc,
    w_in, w_out, w_local, t_in, t_sib, y_out, x_out, s_out, o_in, o_out,
):
    rows, half = tok.shape
    depth, units = gate.shape
    chunks = units // LANES
    piece = rows // PIECES
    row, col = lax.axis_index("row"), lax.axis_index("col")
    yh, z = row // 4, row % 4
    x, yl, core = col // 4, (col // 2) % 2, col % 2
    b = x % 2
    source = (x // 2) == yh
    y = yh * 2 + yl

    def at(x=x, y=y, z=z, core=core):
        return ((y // 2) * 4 + z, x * 4 + (y % 2) * 2 + core)

    z_next, z_prev = (z + 1) % 4, (z + 3) % 4
    x_next, x_prev = (x + 1) % 4, (x + 3) % 4
    right, left = at(z=z_next), at(z=z_prev)
    partner = at(y=(y + 2) % 4)
    flip = at(y=yh * 2 + 1 - yl)
    cross = at(y=(1 - yh) * 2 + 1 - yl)
    sibling = at(core=1 - core)
    pair = at(x=jnp.where(b == 0, x_next, x_prev))
    outer = at(x=jnp.where(b == 0, x_prev, x_next))

    def remote(src, dst, ssem, rsem, to):
        return pltpu.make_async_remote_copy(
            src_ref=src, dst_ref=dst, send_sem=ssem, recv_sem=rsem, device_id=to, device_id_type=MESH
        )

    def lines(m, size=piece):
        return pl.ds(pl.multiple_of(m * size, size), size)

    def landed(ref, sem):
        pltpu.make_async_copy(ref, ref, sem).wait()

    def slot(h, s, lo=0, size=depth):
        return wb.at[h, pl.ds(pl.multiple_of(s * depth + lo, size), size), :]

    def pack(n):
        lane = pl.ds(n * LANES, LANES)
        return (
            pltpu.make_async_copy(gate.at[:, lane], slot(2 * n, z), w_local.at[2 * n]),
            pltpu.make_async_copy(up.at[:, lane], slot(2 * n + 1, z), w_local.at[2 * n + 1]),
        )

    def own_weights(h):
        mine = slot(h, z)
        return (
            remote(mine, mine, w_out.at[h, 0], w_in.at[h, 0], right),
            remote(mine, mine, w_out.at[h, 1], w_in.at[h, 1], left),
        )

    def relayed_weights(h):
        top = slot(h, z_prev, 0, depth // 2)
        low = slot(h, z_next, depth // 2, depth // 2)
        return (
            remote(top, top, w_out.at[h, 2], w_in.at[h, 2], right),
            remote(low, low, w_out.at[h, 3], w_in.at[h, 3], left),
        )

    def start_own(h):
        landed(slot(h, z), w_local.at[h])
        for copy in own_weights(h):
            copy.start()

    def weights_step(h):
        first, second = relayed_weights(h)
        landed(slot(h, z_prev), w_in.at[h, 0])
        first.start()
        landed(slot(h, z_next), w_in.at[h, 1])
        second.start()

        @pl.when(h + 2 < 2 * chunks)
        def _():
            start_own(h + 2)

    def weights_ready(h):
        far = (z + 2) % 4
        landed(slot(h, far, 0, depth // 2), w_in.at[h, 2])
        landed(slot(h, far, depth // 2, depth // 2), w_in.at[h, 3])

    def block(r, p, j, c):
        return tb.at[r, p, j, c]

    def tokens_of(r, p):
        return jnp.concatenate([tb[r, p, j, c] for j in range(4) for c in range(2)], axis=1)

    own_j = b * 2 + yl

    def cross_send(p):
        return remote(tok.at[lines(p), :], block(0, p, own_j, core), y_out.at[0, p], t_in.at[0, p, own_j], cross)

    def flip_send(p):
        return remote(tok.at[lines(p), :], block(1, p, own_j, core), y_out.at[1, p], t_in.at[1, p, own_j], flip)

    def flip_pass(p):
        here = block(0, p, b * 2 + 1 - yl, core)
        return remote(here, here, y_out.at[0, p], t_in.at[0, p, b * 2 + 1 - yl], flip)

    def keep(p):
        return pltpu.make_async_copy(tok.at[lines(p), :], block(1, p, own_j, core), t_in.at[1, p, own_j])

    def cross_step(p):
        @pl.when(jnp.logical_not(source))
        def _():
            if p:
                cross_send(p - 1).wait_send()
            cross_send(p).start()

    def flip_step(p):
        @pl.when(source)
        def _():
            flip_send(p).start()

    def near_j(q):
        return b * 2 + (yl + 1 + q) % 2

    def far_j(q):
        return (1 - b) * 2 + (yl + 1 + q) % 2

    def index(r, p, q):
        return (r * PIECES + p) * 2 + q

    def to_sibling(r, p, j, i, g):
        here = block(r, p, j, core)
        return remote(here, here, s_out.at[i, g], t_sib.at[r, p, j], sibling)

    def outward(r, p, j, i, e, to):
        here = block(r, p, j, core)
        return remote(here, here, x_out.at[i, e], t_in.at[r, p, j], to)

    steps = 4 * PIECES

    def near_step(r, p, q):
        i, j = index(r, p, q), near_j(q)

        @pl.when(source)
        def _():
            landed(block(r, p, j, core), t_in.at[r, p, j])
            outward(r, p, j, i, 0, pair).start()
            outward(r, p, j, i, 1, outer).start()
            if isinstance(r, int) and r == 0 and q == 0:
                flip_pass(p).start()
            to_sibling(r, p, j, i, 0).start()

    def far_step(r, p, q):
        i, j = index(r, p, q), far_j(q)
        landed(block(r, p, j, core), t_in.at[r, p, j])

        @pl.when(jnp.logical_not(source))
        def _():
            outward(r, p, j, i, 0, pair).start()

        to_sibling(r, p, j, i, 1).start()

    def last_step(r, p, q):
        i, j = index(r, p, q), near_j(q)

        @pl.when(jnp.logical_not(source))
        def _():
            landed(block(r, p, j, core), t_in.at[r, p, j])
            to_sibling(r, p, j, i, 0).start()

    def own_rows(k):
        return 1, k % PIECES, 1 - k // PIECES

    def tokens_ready(r):
        @pl.loop(0, PIECES * 4)
        def _(i):
            p, j = i // 4, i % 4
            landed(block(r, p, j, 1 - core), t_sib.at[r, p, j])

    def partial(h, m):
        return remote(send.at[h, lines(m)], got.at[h, lines(m)], o_out.at[h, m], o_in.at[h, m], partner)

    def send_part(h):
        weights_ready(h)

        @pl.loop(0, PIECES)
        def _(m):
            part = jnp.dot(tokens_of(0, m), wb[h], preferred_element_type=jnp.float32)
            send[h, lines(m), :] = encode(part)
            partial(h, m).start()

    def own_part(n):
        @pl.loop(0, PIECES)
        def _(m):
            both = jnp.concatenate([wb[2 * n], wb[2 * n + 1]], axis=1)
            acc[lines(m), :] = jnp.dot(tokens_of(1, m), both, preferred_element_type=jnp.float32)

        @pl.loop(0, PIECES)
        def _(m):
            landed(got.at[2 * n, lines(m)], o_in.at[2 * n, m])
            landed(got.at[2 * n + 1, lines(m)], o_in.at[2 * n + 1, m])

            @pl.loop(m * (piece // 32), (m + 1) * (piece // 32))
            def _(t):
                here = lines(t, 32)
                g = acc[here, :LANES] + decode(got[2 * n, here, :])
                u = acc[here, LANES:] + decode(got[2 * n + 1, here, :])
                out[here, pl.ds(pl.multiple_of(n * LANES, LANES), LANES)] = (g / (1.0 + jnp.exp(-g)) * u).astype(out.dtype)

    for n in range(chunks):
        for copy in pack(n):
            copy.start()

    barrier = pltpu.get_barrier_semaphore()
    neighbours = (right, left, partner, flip, cross, sibling, pair, outer)
    for to in neighbours:
        pl.semaphore_signal(barrier, inc=1, device_id=to, device_id_type=MESH)
    pl.semaphore_wait(barrier, len(neighbours))

    start_own(0)
    cross_step(0)

    @pl.when(source)
    def _():
        for p in range(PIECES):
            keep(p).start()

    start_own(1)

    early = (
        ((cross_step, 1), (near_step, 0, 0, 0), (cross_step, 2), (near_step, 0, 1, 0)),
        ((near_step, 0, 0, 1), (far_step, 0, 0, 0), (near_step, 0, 2, 0), (near_step, 0, 1, 1), (far_step, 0, 1, 0), (last_step, 0, 0, 0)),
        ((near_step, 0, 2, 1), (far_step, 0, 0, 1), (last_step, 0, 1, 0), (flip_step, 0)),
        ((far_step, 0, 2, 0), (last_step, 0, 0, 1), (flip_step, 1), (far_step, 0, 1, 1), (last_step, 0, 2, 0), (flip_step, 2)),
        ((near_step, *own_rows(0)), (far_step, 0, 2, 1), (last_step, 0, 1, 1), (near_step, *own_rows(1))),
        ((far_step, *own_rows(0)), (last_step, 0, 2, 1), (near_step, *own_rows(2))),
    )
    for h, events in enumerate(early):
        weights_step(h)
        for event, *which in events:
            event(*which)
    tokens_ready(0)
    late = len(early)

    @pl.loop(late, 2 * chunks + 1)
    def _(h):
        @pl.when(h < 2 * chunks)
        def _():
            weights_step(h)

        @pl.when(h <= 8)
        def _():
            near_step(*own_rows(h - 3))

        @pl.loop(jnp.minimum(h - 5 + jnp.where(h >= 8, 1, 0), 6), jnp.minimum(h - 4 + jnp.where(h >= 7, 1, 0), 6))
        def _(k):
            far_step(*own_rows(k))

        @pl.loop(jnp.minimum(h - 6 + jnp.where(h >= 9, 1, 0), 6), jnp.minimum(h - 5 + jnp.where(h >= 8, 1, 0), 6))
        def _(k):
            last_step(*own_rows(k))

        @pl.when(h == 10)
        def _():
            tokens_ready(1)

        @pl.loop(jnp.where(h == late, 0, jnp.minimum(2 * h - 11, h - 1)), jnp.minimum(2 * h - 9, h))
        def _(s):
            send_part(s)

        @pl.loop(jnp.clip(2 * (h - 10), 0, jnp.maximum(h - 8, 0)), jnp.clip(2 * (h - 9), 0, jnp.maximum(h - 7, 0)))
        def _(n):
            own_part(n)

    @pl.loop(0, 2 * chunks)
    def _(h):
        for copy in own_weights(h) + relayed_weights(h):
            copy.wait_send()

        @pl.loop(0, PIECES)
        def _(m):
            partial(h, m).wait_send()

    for p in range(PIECES):
        @pl.when(source)
        def _():
            flip_pass(p).wait_send()
            flip_send(p).wait_send()

    @pl.when(jnp.logical_not(source))
    def _():
        cross_send(PIECES - 1).wait_send()

    @pl.loop(0, steps)
    def _(i):
        r, p, j = i // (2 * PIECES), (i // 2) % PIECES, b * 2
        outward(r, p, j, i, 0, pair).wait_send()
        to_sibling(r, p, j, i, 0).wait_send()
        to_sibling(r, p, j, i, 1).wait_send()

        @pl.when(source)
        def _():
            outward(r, p, j, i, 1, outer).wait_send()


def on_device(tokens, gate_weight, up_weight):
    rows, half = tokens.shape
    depth, units = gate_weight.shape
    chunks = units // LANES
    dma = pltpu.SemaphoreType.DMA
    return pl.pallas_call(
        kernel,
        out_shape=jax.ShapeDtypeStruct((rows, units), jnp.bfloat16),
        in_specs=[pl.BlockSpec(memory_space=pl.ANY)] * 3,
        out_specs=pl.BlockSpec(memory_space=pltpu.VMEM),
        scratch_shapes=[
            pltpu.VMEM((2 * chunks, 4 * depth, LANES), jnp.bfloat16),
            pltpu.VMEM((2, PIECES, 4, 2, rows // PIECES, half), jnp.bfloat16),
            pltpu.VMEM((2 * chunks, rows, LANES), jnp.bfloat16),
            pltpu.VMEM((2 * chunks, rows, LANES), jnp.bfloat16),
            pltpu.VMEM((rows, 2 * LANES), jnp.float32),
            dma((2 * chunks, 4)),
            dma((2 * chunks, 4)),
            dma((2 * chunks,)),
            dma((2, PIECES, 4)),
            dma((2, PIECES, 4)),
            dma((2, PIECES)),
            dma((4 * PIECES, 2)),
            dma((4 * PIECES, 2)),
            dma((2 * chunks, PIECES)),
            dma((2 * chunks, PIECES)),
        ],
        compiler_params=pltpu.CompilerParams(
            collective_id=0, has_side_effects=True, vmem_limit_bytes=60 * 2**20
        ),
        cost_estimate=pl.CostEstimate(
            flops=2 * rows * 16 * half * units * 2, bytes_accessed=2 * (rows * half + 2 * depth * units + rows * units), transcendentals=0
        ),
    )(tokens, gate_weight, up_weight)


def solution(mesh):
    placed = (P("row", "col"), P("row", "col"), P("row", "col"))
    return jax.shard_map(
        on_device, mesh=mesh, in_specs=placed, out_specs=P("row", "col"), check_vma=False
    )
```

```python
import functools

import jax
import jax.numpy as jnp
from jax import lax
from jax.experimental import pallas as pl
from jax.experimental.pallas import tpu as pltpu
from jax.sharding import PartitionSpec as P

MESH = pl.DeviceIdType.MESH
LANES = 128
PIECES = 3


def encode(v):
    w = v * 2.0**14
    w2 = w * w
    return (w2 * w2 * w).astype(jnp.bfloat16)


def decode(u):
    u = u.astype(jnp.float32)
    r = jnp.exp2(jnp.log2(jnp.abs(u)) * 0.2 - 14.0)
    return jnp.where(u < 0, -r, r)


def kernel(
    tok, gate, up, out_hbm,
    wb, tb, send, got, acc, out,
    w_in, w_out, w_local, t_in, t_sib, y_out, x_out, s_out, o_in, o_out, done,
):
    rows, half = tok.shape
    depth, units = gate.shape
    chunks = units // LANES
    piece = rows // PIECES
    row, col = lax.axis_index("row"), lax.axis_index("col")
    yh, z = row // 4, row % 4
    x, yl, core = col // 4, (col // 2) % 2, col % 2
    b = x % 2
    source = (x // 2) == yh
    y = yh * 2 + yl

    def at(x=x, y=y, z=z, core=core):
        return ((y // 2) * 4 + z, x * 4 + (y % 2) * 2 + core)

    z_next, z_prev = (z + 1) % 4, (z + 3) % 4
    x_next, x_prev = (x + 1) % 4, (x + 3) % 4
    right, left = at(z=z_next), at(z=z_prev)
    partner = at(y=(y + 2) % 4)
    flip = at(y=yh * 2 + 1 - yl)
    cross = at(y=(1 - yh) * 2 + 1 - yl)
    sibling = at(core=1 - core)
    pair = at(x=jnp.where(b == 0, x_next, x_prev))
    outer = at(x=jnp.where(b == 0, x_prev, x_next))

    def remote(src, dst, ssem, rsem, to):
        return pltpu.make_async_remote_copy(
            src_ref=src, dst_ref=dst, send_sem=ssem, recv_sem=rsem, device_id=to, device_id_type=MESH
        )

    def lines(m, size=piece):
        return pl.ds(pl.multiple_of(m * size, size), size)

    def landed(ref, sem):
        pltpu.make_async_copy(ref, ref, sem).wait()

    def slot(h, s, lo=0, size=depth):
        return wb.at[h, pl.ds(pl.multiple_of(s * depth + lo, size), size), :]

    def pack(n):
        lane = pl.ds(n * LANES, LANES)
        return (
            pltpu.make_async_copy(gate.at[:, lane], slot(2 * n, z), w_local.at[2 * n]),
            pltpu.make_async_copy(up.at[:, lane], slot(2 * n + 1, z), w_local.at[2 * n + 1]),
        )

    def first_half(h):
        top, low = slot(h, z, 0, depth // 2), slot(h, z, depth // 2, depth // 2)
        return (
            remote(top, top, w_out.at[h, 0], w_in.at[h, 0], right),
            remote(low, low, w_out.at[h, 1], w_in.at[h, 1], left),
        )

    def second_half(h):
        top, low = slot(h, z, 0, depth // 2), slot(h, z, depth // 2, depth // 2)
        return (
            remote(low, low, w_out.at[h, 2], w_in.at[h, 2], right),
            remote(top, top, w_out.at[h, 3], w_in.at[h, 3], left),
        )

    def relayed(h):
        top = slot(h, z_prev, 0, depth // 2)
        low = slot(h, z_next, depth // 2, depth // 2)
        return (
            remote(top, top, w_out.at[h, 4], w_in.at[h, 4], right),
            remote(low, low, w_out.at[h, 5], w_in.at[h, 5], left),
        )

    def start_first(h):
        landed(slot(h, z), w_local.at[h])
        for copy in first_half(h):
            copy.start()

    def start_second(h):
        for copy in second_half(h):
            copy.start()

    def weights_step(h):
        first, second = relayed(h)
        landed(slot(h, z_prev, 0, depth // 2), w_in.at[h, 0])
        first.start()
        landed(slot(h, z_next, depth // 2, depth // 2), w_in.at[h, 1])
        second.start()

        @pl.when(h + 1 < 2 * chunks)
        def _():
            start_second(h + 1)

        @pl.when(h + 2 < 2 * chunks)
        def _():
            start_first(h + 2)

    def weights_ready(h):
        far = (z + 2) % 4
        landed(slot(h, z_prev, depth // 2, depth // 2), w_in.at[h, 2])
        landed(slot(h, z_next, 0, depth // 2), w_in.at[h, 3])
        landed(slot(h, far, 0, depth // 2), w_in.at[h, 4])
        landed(slot(h, far, depth // 2, depth // 2), w_in.at[h, 5])

    def block(r, p, j, c):
        return tb.at[r, p, j, c]

    def tokens_of(r, p):
        return jnp.concatenate([tb[r, p, j, c] for j in range(4) for c in range(2)], axis=1)

    own_j = b * 2 + yl

    def cross_send(p):
        return remote(tok.at[lines(p), :], block(0, p, own_j, core), y_out.at[0, p], t_in.at[0, p, own_j], cross)

    def flip_send(p):
        return remote(tok.at[lines(p), :], block(1, p, own_j, core), y_out.at[1, p], t_in.at[1, p, own_j], flip)

    def flip_pass(p):
        here = block(0, p, b * 2 + 1 - yl, core)
        return remote(here, here, y_out.at[0, p], t_in.at[0, p, b * 2 + 1 - yl], flip)

    def keep(p):
        return pltpu.make_async_copy(tok.at[lines(p), :], block(1, p, own_j, core), t_in.at[1, p, own_j])

    def cross_step(p):
        @pl.when(jnp.logical_not(source))
        def _():
            if p:
                cross_send(p - 1).wait_send()
            cross_send(p).start()

    def flip_step(p):
        @pl.when(source)
        def _():
            flip_send(p).start()

    def near_j(q):
        return b * 2 + (yl + 1 + q) % 2

    def far_j(q):
        return (1 - b) * 2 + (yl + 1 + q) % 2

    def index(r, p, q):
        return (r * PIECES + p) * 2 + q

    def to_sibling(r, p, j, i, g):
        here = block(r, p, j, core)
        return remote(here, here, s_out.at[i, g], t_sib.at[r, p, j], sibling)

    def outward(r, p, j, i, e, to):
        here = block(r, p, j, core)
        return remote(here, here, x_out.at[i, e], t_in.at[r, p, j], to)

    steps = 4 * PIECES

    def near_step(r, p, q):
        i, j = index(r, p, q), near_j(q)

        @pl.when(source)
        def _():
            landed(block(r, p, j, core), t_in.at[r, p, j])
            outward(r, p, j, i, 0, pair).start()
            outward(r, p, j, i, 1, outer).start()
            if isinstance(r, int) and r == 0 and q == 0:
                flip_pass(p).start()
            to_sibling(r, p, j, i, 0).start()

    def far_step(r, p, q):
        i, j = index(r, p, q), far_j(q)
        landed(block(r, p, j, core), t_in.at[r, p, j])

        @pl.when(jnp.logical_not(source))
        def _():
            outward(r, p, j, i, 0, pair).start()

        to_sibling(r, p, j, i, 1).start()

    def last_step(r, p, q):
        i, j = index(r, p, q), near_j(q)

        @pl.when(jnp.logical_not(source))
        def _():
            landed(block(r, p, j, core), t_in.at[r, p, j])
            to_sibling(r, p, j, i, 0).start()

    def own_rows(k):
        return 1, k % PIECES, 1 - k // PIECES

    def tokens_ready(r):
        @pl.loop(0, PIECES * 4)
        def _(i):
            p, j = i // 4, i % 4
            landed(block(r, p, j, 1 - core), t_sib.at[r, p, j])

    def partial(h, m):
        return remote(send.at[h, lines(m)], got.at[h, lines(m)], o_out.at[h, m], o_in.at[h, m], partner)

    def send_part(h):
        weights_ready(h)

        @pl.loop(0, PIECES)
        def _(m):
            part = jnp.dot(tokens_of(0, m), wb[h], preferred_element_type=jnp.float32)
            send[h, lines(m), :] = encode(part)
            partial(h, m).start()

    def own_part(n):
        @pl.loop(0, PIECES)
        def _(m):
            both = jnp.concatenate([wb[2 * n], wb[2 * n + 1]], axis=1)
            acc[lines(m), :] = jnp.dot(tokens_of(1, m), both, preferred_element_type=jnp.float32)

        @pl.loop(0, PIECES)
        def _(m):
            landed(got.at[2 * n, lines(m)], o_in.at[2 * n, m])
            landed(got.at[2 * n + 1, lines(m)], o_in.at[2 * n + 1, m])

            @pl.loop(m * (piece // 32), (m + 1) * (piece // 32))
            def _(t):
                here = lines(t, 32)
                g = acc[here, :LANES] + decode(got[2 * n, here, :])
                u = acc[here, LANES:] + decode(got[2 * n + 1, here, :])
                out[n, here, :] = (g / (1.0 + jnp.exp(-g)) * u).astype(out.dtype)

            result(n, m).start()

    def result(n, m):
        lane = pl.ds(pl.multiple_of(n * LANES, LANES), LANES)
        return pltpu.make_async_copy(out.at[n, lines(m)], out_hbm.at[lines(m), lane], done.at[n, m])

    for n in range(chunks):
        for copy in pack(n):
            copy.start()

    barrier = pltpu.get_barrier_semaphore()
    neighbours = (right, left, partner, flip, cross, sibling, pair, outer)
    for to in neighbours:
        pl.semaphore_signal(barrier, inc=1, device_id=to, device_id_type=MESH)
    pl.semaphore_wait(barrier, len(neighbours))

    start_first(0)
    start_second(0)
    cross_step(0)

    @pl.when(source)
    def _():
        for p in range(PIECES):
            keep(p).start()

    start_first(1)

    early = (
        ((cross_step, 1), (near_step, 0, 0, 0), (cross_step, 2), (near_step, 0, 1, 0)),
        ((near_step, 0, 0, 1), (far_step, 0, 0, 0), (near_step, 0, 2, 0), (near_step, 0, 1, 1), (far_step, 0, 1, 0), (last_step, 0, 0, 0)),
        ((near_step, 0, 2, 1), (far_step, 0, 0, 1), (last_step, 0, 1, 0), (flip_step, 0)),
        ((far_step, 0, 2, 0), (last_step, 0, 0, 1), (flip_step, 1), (far_step, 0, 1, 1), (last_step, 0, 2, 0), (flip_step, 2)),
        ((near_step, *own_rows(0)), (far_step, 0, 2, 1), (last_step, 0, 1, 1), (near_step, *own_rows(1))),
        ((far_step, *own_rows(0)), (last_step, 0, 2, 1), (near_step, *own_rows(2))),
    )
    for h, events in enumerate(early):
        weights_step(h)
        for event, *which in events:
            event(*which)
    tokens_ready(0)
    late = len(early)

    @pl.loop(late, 2 * chunks + 1)
    def _(h):
        @pl.when(h < 2 * chunks)
        def _():
            weights_step(h)

        @pl.when(h <= 8)
        def _():
            near_step(*own_rows(h - 3))

        @pl.loop(jnp.minimum(h - 5 + jnp.where(h >= 8, 1, 0), 6), jnp.minimum(h - 4 + jnp.where(h >= 7, 1, 0), 6))
        def _(k):
            far_step(*own_rows(k))

        @pl.loop(jnp.minimum(h - 6 + jnp.where(h >= 9, 1, 0), 6), jnp.minimum(h - 5 + jnp.where(h >= 8, 1, 0), 6))
        def _(k):
            last_step(*own_rows(k))

        @pl.when(h == 10)
        def _():
            tokens_ready(1)

        @pl.loop(jnp.where(h == late, 0, jnp.minimum(2 * h - 11, h - 1)), jnp.minimum(2 * h - 9, h))
        def _(s):
            send_part(s)

        @pl.loop(jnp.clip(2 * (h - 10), 0, jnp.maximum(h - 8, 0)), jnp.clip(2 * (h - 9), 0, jnp.maximum(h - 7, 0)))
        def _(n):
            own_part(n)

    @pl.loop(0, 2 * chunks)
    def _(h):
        for copy in first_half(h) + second_half(h) + relayed(h):
            copy.wait_send()

        @pl.loop(0, PIECES)
        def _(m):
            partial(h, m).wait_send()

    @pl.loop(0, chunks)
    def _(n):
        @pl.loop(0, PIECES)
        def _(m):
            result(n, m).wait()

    for p in range(PIECES):
        @pl.when(source)
        def _():
            flip_pass(p).wait_send()
            flip_send(p).wait_send()

    @pl.when(jnp.logical_not(source))
    def _():
        cross_send(PIECES - 1).wait_send()

    @pl.loop(0, steps)
    def _(i):
        r, p, j = i // (2 * PIECES), (i // 2) % PIECES, b * 2
        outward(r, p, j, i, 0, pair).wait_send()
        to_sibling(r, p, j, i, 0).wait_send()
        to_sibling(r, p, j, i, 1).wait_send()

        @pl.when(source)
        def _():
            outward(r, p, j, i, 1, outer).wait_send()


def on_device(tokens, gate_weight, up_weight):
    rows, half = tokens.shape
    depth, units = gate_weight.shape
    chunks = units // LANES
    dma = pltpu.SemaphoreType.DMA
    return pl.pallas_call(
        kernel,
        out_shape=jax.ShapeDtypeStruct((rows, units), jnp.bfloat16),
        in_specs=[pl.BlockSpec(memory_space=pl.ANY)] * 3,
        out_specs=pl.BlockSpec(memory_space=pl.ANY),
        scratch_shapes=[
            pltpu.VMEM((2 * chunks, 4 * depth, LANES), jnp.bfloat16),
            pltpu.VMEM((2, PIECES, 4, 2, rows // PIECES, half), jnp.bfloat16),
            pltpu.VMEM((2 * chunks, rows, LANES), jnp.bfloat16),
            pltpu.VMEM((2 * chunks, rows, LANES), jnp.bfloat16),
            pltpu.VMEM((rows, 2 * LANES), jnp.float32),
            pltpu.VMEM((chunks, rows, LANES), jnp.bfloat16),
            dma((2 * chunks, 6)),
            dma((2 * chunks, 6)),
            dma((2 * chunks,)),
            dma((2, PIECES, 4)),
            dma((2, PIECES, 4)),
            dma((2, PIECES)),
            dma((4 * PIECES, 2)),
            dma((4 * PIECES, 2)),
            dma((2 * chunks, PIECES)),
            dma((2 * chunks, PIECES)),
            dma((chunks, PIECES)),
        ],
        compiler_params=pltpu.CompilerParams(
            collective_id=0, has_side_effects=True, vmem_limit_bytes=60 * 2**20
        ),
        cost_estimate=pl.CostEstimate(
            flops=2 * rows * 16 * half * units * 2, bytes_accessed=2 * (rows * half + 2 * depth * units + rows * units), transcendentals=0
        ),
    )(tokens, gate_weight, up_weight)


def solution(mesh):
    placed = (P("row", "col"), P("row", "col"), P("row", "col"))
    return jax.shard_map(
        on_device, mesh=mesh, in_specs=placed, out_specs=P("row", "col"), check_vma=False
    )
```

```python
import functools

import jax
import jax.numpy as jnp
from jax import lax
from jax.experimental import pallas as pl
from jax.experimental.pallas import tpu as pltpu
from jax.sharding import PartitionSpec as P

MESH = pl.DeviceIdType.MESH
LANES = 128
PIECES = 3


def encode(v):
    w = v * 2.0**14
    w2 = w * w
    return (w2 * w2 * w).astype(jnp.bfloat16)


def decode(u):
    u = u.astype(jnp.float32)
    r = jnp.exp2(jnp.log2(jnp.abs(u)) * 0.2 - 14.0)
    return jnp.where(u < 0, -r, r)


def kernel(
    tok, gate, up, hidden, last_own, last_got,
    wb, tb, send, got, acc, out,
    w_in, w_out, w_local, t_in, t_sib, y_out, x_out, s_out, o_in, o_out, done, kept,
):
    rows, half = tok.shape
    depth, units = gate.shape
    chunks = units // LANES
    piece = rows // PIECES
    row, col = lax.axis_index("row"), lax.axis_index("col")
    yh, z = row // 4, row % 4
    x, yl, core = col // 4, (col // 2) % 2, col % 2
    b = x % 2
    source = (x // 2) == yh
    y = yh * 2 + yl

    def at(x=x, y=y, z=z, core=core):
        return ((y // 2) * 4 + z, x * 4 + (y % 2) * 2 + core)

    z_next, z_prev = (z + 1) % 4, (z + 3) % 4
    x_next, x_prev = (x + 1) % 4, (x + 3) % 4
    right, left = at(z=z_next), at(z=z_prev)
    partner = at(y=(y + 2) % 4)
    flip = at(y=yh * 2 + 1 - yl)
    cross = at(y=(1 - yh) * 2 + 1 - yl)
    sibling = at(core=1 - core)
    pair = at(x=jnp.where(b == 0, x_next, x_prev))
    outer = at(x=jnp.where(b == 0, x_prev, x_next))

    def remote(src, dst, ssem, rsem, to):
        return pltpu.make_async_remote_copy(
            src_ref=src, dst_ref=dst, send_sem=ssem, recv_sem=rsem, device_id=to, device_id_type=MESH
        )

    def lines(m, size=piece):
        return pl.ds(pl.multiple_of(m * size, size), size)

    def landed(ref, sem):
        pltpu.make_async_copy(ref, ref, sem).wait()

    def slot(h, s, lo=0, size=depth):
        return wb.at[h, pl.ds(pl.multiple_of(s * depth + lo, size), size), :]

    def pack(n):
        lane = pl.ds(n * LANES, LANES)
        return (
            pltpu.make_async_copy(gate.at[:, lane], slot(2 * n, z), w_local.at[2 * n]),
            pltpu.make_async_copy(up.at[:, lane], slot(2 * n + 1, z), w_local.at[2 * n + 1]),
        )

    def first_half(h):
        top, low = slot(h, z, 0, depth // 2), slot(h, z, depth // 2, depth // 2)
        return (
            remote(top, top, w_out.at[h, 0], w_in.at[h, 0], right),
            remote(low, low, w_out.at[h, 1], w_in.at[h, 1], left),
        )

    def second_half(h):
        top, low = slot(h, z, 0, depth // 2), slot(h, z, depth // 2, depth // 2)
        return (
            remote(low, low, w_out.at[h, 2], w_in.at[h, 2], right),
            remote(top, top, w_out.at[h, 3], w_in.at[h, 3], left),
        )

    def relayed(h):
        top = slot(h, z_prev, 0, depth // 2)
        low = slot(h, z_next, depth // 2, depth // 2)
        return (
            remote(top, top, w_out.at[h, 4], w_in.at[h, 4], right),
            remote(low, low, w_out.at[h, 5], w_in.at[h, 5], left),
        )

    def start_first(h):
        landed(slot(h, z), w_local.at[h])
        for copy in first_half(h):
            copy.start()

    def start_second(h):
        for copy in second_half(h):
            copy.start()

    def weights_step(h):
        first, second = relayed(h)
        landed(slot(h, z_prev, 0, depth // 2), w_in.at[h, 0])
        first.start()
        landed(slot(h, z_next, depth // 2, depth // 2), w_in.at[h, 1])
        second.start()

        @pl.when(h + 1 < 2 * chunks)
        def _():
            start_second(h + 1)

        @pl.when(h + 2 < 2 * chunks)
        def _():
            start_first(h + 2)

    def weights_ready(h):
        far = (z + 2) % 4
        landed(slot(h, z_prev, depth // 2, depth // 2), w_in.at[h, 2])
        landed(slot(h, z_next, 0, depth // 2), w_in.at[h, 3])
        landed(slot(h, far, 0, depth // 2), w_in.at[h, 4])
        landed(slot(h, far, depth // 2, depth // 2), w_in.at[h, 5])

    def block(r, p, j, c):
        return tb.at[r, p, j, c]

    def tokens_of(r, p):
        return jnp.concatenate([tb[r, p, j, c] for j in range(4) for c in range(2)], axis=1)

    own_j = b * 2 + yl

    def cross_send(p):
        return remote(tok.at[lines(p), :], block(0, p, own_j, core), y_out.at[0, p], t_in.at[0, p, own_j], cross)

    def flip_send(p):
        return remote(tok.at[lines(p), :], block(1, p, own_j, core), y_out.at[1, p], t_in.at[1, p, own_j], flip)

    def flip_pass(p):
        here = block(0, p, b * 2 + 1 - yl, core)
        return remote(here, here, y_out.at[0, p], t_in.at[0, p, b * 2 + 1 - yl], flip)

    def keep(p):
        return pltpu.make_async_copy(tok.at[lines(p), :], block(1, p, own_j, core), t_in.at[1, p, own_j])

    def cross_step(p):
        @pl.when(jnp.logical_not(source))
        def _():
            if p:
                cross_send(p - 1).wait_send()
            cross_send(p).start()

    def flip_step(p):
        @pl.when(source)
        def _():
            flip_send(p).start()

    def near_j(q):
        return b * 2 + (yl + 1 + q) % 2

    def far_j(q):
        return (1 - b) * 2 + (yl + 1 + q) % 2

    def index(r, p, q):
        return (r * PIECES + p) * 2 + q

    def to_sibling(r, p, j, i, g):
        here = block(r, p, j, core)
        return remote(here, here, s_out.at[i, g], t_sib.at[r, p, j], sibling)

    def outward(r, p, j, i, e, to):
        here = block(r, p, j, core)
        return remote(here, here, x_out.at[i, e], t_in.at[r, p, j], to)

    steps = 4 * PIECES

    def near_step(r, p, q):
        i, j = index(r, p, q), near_j(q)

        @pl.when(source)
        def _():
            landed(block(r, p, j, core), t_in.at[r, p, j])
            outward(r, p, j, i, 0, pair).start()
            outward(r, p, j, i, 1, outer).start()
            if isinstance(r, int) and r == 0 and q == 0:
                flip_pass(p).start()
            to_sibling(r, p, j, i, 0).start()

    def far_step(r, p, q):
        i, j = index(r, p, q), far_j(q)
        landed(block(r, p, j, core), t_in.at[r, p, j])

        @pl.when(jnp.logical_not(source))
        def _():
            outward(r, p, j, i, 0, pair).start()

        to_sibling(r, p, j, i, 1).start()

    def last_step(r, p, q):
        i, j = index(r, p, q), near_j(q)

        @pl.when(jnp.logical_not(source))
        def _():
            landed(block(r, p, j, core), t_in.at[r, p, j])
            to_sibling(r, p, j, i, 0).start()

    def own_rows(k):
        return 1, k % PIECES, 1 - k // PIECES

    def tokens_ready(r):
        @pl.loop(0, PIECES * 4)
        def _(i):
            p, j = i // 4, i % 4
            landed(block(r, p, j, 1 - core), t_sib.at[r, p, j])

    last = 2 * chunks - 2

    def partial(h, m):
        return remote(send.at[h, lines(m)], got.at[h, lines(m)], o_out.at[h, m], o_in.at[h, m], partner)

    def last_partial(g, m):
        h = last + g
        return remote(send.at[h, lines(m)], last_got.at[g, lines(m)], o_out.at[h, m], o_in.at[h, m], partner)

    def send_part(h):
        weights_ready(h)

        @pl.loop(0, PIECES)
        def _(m):
            part = jnp.dot(tokens_of(0, m), wb[h], preferred_element_type=jnp.float32)
            send[h, lines(m), :] = encode(part)

            @pl.when(h < last)
            def _():
                partial(h, m).start()

            @pl.when(h == last)
            def _():
                last_partial(0, m).start()

    def last_send_part():
        h = 2 * chunks - 1
        far = (z + 2) % 4
        landed(slot(h, z_prev, depth // 2, depth // 2), w_in.at[h, 2])
        landed(slot(h, z_next, 0, depth // 2), w_in.at[h, 3])

        def some(m, s):
            rows_of = jnp.concatenate([tb[0, m, s, c] for c in range(2)], axis=1)
            return jnp.dot(rows_of, wb[h, pl.ds(pl.multiple_of(s * depth, depth), depth), :], preferred_element_type=jnp.float32)

        @pl.loop(0, PIECES)
        def _(m):
            acc[lines(m), :LANES] = some(m, z) + some(m, z_prev) + some(m, z_next)

        landed(slot(h, far, 0, depth // 2), w_in.at[h, 4])
        landed(slot(h, far, depth // 2, depth // 2), w_in.at[h, 5])

        @pl.loop(0, PIECES)
        def _(m):
            send[h, lines(m), :] = encode(acc[lines(m), :LANES] + some(m, far))
            last_partial(1, m).start()

    def last_own_part():
        @pl.loop(0, PIECES)
        def _(m):
            both = jnp.concatenate([wb[last], wb[last + 1]], axis=1)
            acc[lines(m), :] = jnp.dot(tokens_of(1, m), both, preferred_element_type=jnp.float32)
            kept_sums(m).start()

    def kept_sums(m):
        return pltpu.make_async_copy(acc.at[lines(m)], last_own.at[lines(m)], kept.at[m])

    def own_part(n):
        @pl.loop(0, PIECES)
        def _(m):
            both = jnp.concatenate([wb[2 * n], wb[2 * n + 1]], axis=1)
            acc[lines(m), :] = jnp.dot(tokens_of(1, m), both, preferred_element_type=jnp.float32)

        @pl.loop(0, PIECES)
        def _(m):
            landed(got.at[2 * n, lines(m)], o_in.at[2 * n, m])
            landed(got.at[2 * n + 1, lines(m)], o_in.at[2 * n + 1, m])

            @pl.loop(m * (piece // 32), (m + 1) * (piece // 32))
            def _(t):
                here = lines(t, 32)
                g = acc[here, :LANES] + decode(got[2 * n, here, :])
                u = acc[here, LANES:] + decode(got[2 * n + 1, here, :])
                out[n, here, :] = (g / (1.0 + jnp.exp(-g)) * u).astype(out.dtype)

            result(n, m).start()

    def result(n, m):
        lane = pl.ds(pl.multiple_of(n * LANES, LANES), LANES)
        return pltpu.make_async_copy(out.at[n, lines(m)], hidden.at[lines(m), lane], done.at[n, m])

    for n in range(chunks):
        for copy in pack(n):
            copy.start()

    barrier = pltpu.get_barrier_semaphore()
    neighbours = (right, left, partner, flip, cross, sibling, pair, outer)
    for to in neighbours:
        pl.semaphore_signal(barrier, inc=1, device_id=to, device_id_type=MESH)
    pl.semaphore_wait(barrier, len(neighbours))

    start_first(0)
    start_second(0)
    cross_step(0)

    @pl.when(source)
    def _():
        for p in range(PIECES):
            keep(p).start()

    start_first(1)

    early = (
        ((cross_step, 1), (near_step, 0, 0, 0), (cross_step, 2), (near_step, 0, 1, 0)),
        ((near_step, 0, 0, 1), (far_step, 0, 0, 0), (near_step, 0, 2, 0), (near_step, 0, 1, 1), (far_step, 0, 1, 0), (last_step, 0, 0, 0)),
        ((near_step, 0, 2, 1), (far_step, 0, 0, 1), (last_step, 0, 1, 0), (flip_step, 0)),
        ((far_step, 0, 2, 0), (last_step, 0, 0, 1), (flip_step, 1), (far_step, 0, 1, 1), (last_step, 0, 2, 0), (flip_step, 2)),
        ((near_step, *own_rows(0)), (far_step, 0, 2, 1), (last_step, 0, 1, 1), (near_step, *own_rows(1))),
        ((far_step, *own_rows(0)), (last_step, 0, 2, 1), (near_step, *own_rows(2))),
    )
    for h, events in enumerate(early):
        weights_step(h)
        for event, *which in events:
            event(*which)
    tokens_ready(0)
    late = len(early)

    @pl.loop(late, 2 * chunks)
    def _(h):
        weights_step(h)

        @pl.when(h <= 8)
        def _():
            near_step(*own_rows(h - 3))

        @pl.loop(jnp.minimum(h - 5 + jnp.where(h >= 8, 1, 0), 6), jnp.minimum(h - 4 + jnp.where(h >= 7, 1, 0), 6))
        def _(k):
            far_step(*own_rows(k))

        @pl.loop(jnp.minimum(h - 6 + jnp.where(h >= 9, 1, 0), 6), jnp.minimum(h - 5 + jnp.where(h >= 8, 1, 0), 6))
        def _(k):
            last_step(*own_rows(k))

        @pl.when(h == 10)
        def _():
            tokens_ready(1)

        @pl.loop(jnp.where(h == late, 0, jnp.minimum(2 * h - 11, h - 1)), jnp.minimum(2 * h - 9, h))
        def _(s):
            send_part(s)

        @pl.loop(jnp.clip(2 * (h - 10), 0, jnp.clip(h - 8, 0, 5)), jnp.where(h == 13, 5, jnp.clip(2 * (h - 9), 0, jnp.maximum(h - 7, 0))))
        def _(n):
            own_part(n)

    last_send_part()
    own_part(chunks - 2)
    last_own_part()

    @pl.loop(0, 2 * chunks)
    def _(h):
        for copy in first_half(h) + second_half(h) + relayed(h):
            copy.wait_send()

        @pl.when(h < last)
        def _():
            @pl.loop(0, PIECES)
            def _(m):
                partial(h, m).wait_send()

    @pl.loop(0, chunks - 1)
    def _(n):
        @pl.loop(0, PIECES)
        def _(m):
            result(n, m).wait()

    for p in range(PIECES):
        @pl.when(source)
        def _():
            flip_pass(p).wait_send()
            flip_send(p).wait_send()

    @pl.when(jnp.logical_not(source))
    def _():
        cross_send(PIECES - 1).wait_send()

    @pl.loop(0, steps)
    def _(i):
        r, p, j = i // (2 * PIECES), (i // 2) % PIECES, b * 2
        outward(r, p, j, i, 0, pair).wait_send()
        to_sibling(r, p, j, i, 0).wait_send()
        to_sibling(r, p, j, i, 1).wait_send()

        @pl.when(source)
        def _():
            outward(r, p, j, i, 1, outer).wait_send()

    for m in range(PIECES):
        kept_sums(m).wait()
        for g in range(2):
            last_partial(g, m).wait_send()
            landed(last_got.at[g, lines(m)], o_in.at[last + g, m])


def closing(hidden, last_own, last_got, out, whole, own, got, sem_in, sem_out):
    rows, units = out.shape
    piece = rows // PIECES
    known = units - LANES

    def lines(m):
        return pl.ds(m * piece, piece)

    def loads(m):
        return (
            pltpu.make_async_copy(last_own.at[lines(m)], own.at[lines(m)], sem_in.at[m, 0]),
            pltpu.make_async_copy(last_got.at[0, lines(m)], got.at[0, lines(m)], sem_in.at[m, 1]),
            pltpu.make_async_copy(last_got.at[1, lines(m)], got.at[1, lines(m)], sem_in.at[m, 2]),
            pltpu.make_async_copy(hidden.at[lines(m)], whole.at[lines(m), pl.ds(0, known)], sem_in.at[m, 3]),
        )

    def store(m):
        return pltpu.make_async_copy(whole.at[lines(m)], out.at[lines(m)], sem_out.at[m])

    for m in range(PIECES):
        for copy in loads(m):
            copy.start()
    for m in range(PIECES):
        for copy in loads(m):
            copy.wait()

        @pl.loop(m * (piece // 32), (m + 1) * (piece // 32))
        def _(t):
            here = pl.ds(pl.multiple_of(t * 32, 32), 32)
            g = own[here, :LANES] + decode(got[0, here, :])
            u = own[here, LANES:] + decode(got[1, here, :])
            whole[here, pl.ds(known, LANES)] = (g / (1.0 + jnp.exp(-g)) * u).astype(out.dtype)

        store(m).start()
    for m in range(PIECES):
        store(m).wait()


def on_device(tokens, gate_weight, up_weight):
    rows, half = tokens.shape
    depth, units = gate_weight.shape
    chunks = units // LANES
    dma = pltpu.SemaphoreType.DMA
    any_space = pl.BlockSpec(memory_space=pl.ANY)
    parts = pl.pallas_call(
        kernel,
        out_shape=(
            jax.ShapeDtypeStruct((rows, units - LANES), jnp.bfloat16),
            jax.ShapeDtypeStruct((rows, 2 * LANES), jnp.float32),
            jax.ShapeDtypeStruct((2, rows, LANES), jnp.bfloat16),
        ),
        in_specs=[any_space] * 3,
        out_specs=(any_space,) * 3,
        scratch_shapes=[
            pltpu.VMEM((2 * chunks, 4 * depth, LANES), jnp.bfloat16),
            pltpu.VMEM((2, PIECES, 4, 2, rows // PIECES, half), jnp.bfloat16),
            pltpu.VMEM((2 * chunks, rows, LANES), jnp.bfloat16),
            pltpu.VMEM((2 * chunks, rows, LANES), jnp.bfloat16),
            pltpu.VMEM((rows, 2 * LANES), jnp.float32),
            pltpu.VMEM((chunks, rows, LANES), jnp.bfloat16),
            dma((2 * chunks, 6)),
            dma((2 * chunks, 6)),
            dma((2 * chunks,)),
            dma((2, PIECES, 4)),
            dma((2, PIECES, 4)),
            dma((2, PIECES)),
            dma((4 * PIECES, 2)),
            dma((4 * PIECES, 2)),
            dma((2 * chunks, PIECES)),
            dma((2 * chunks, PIECES)),
            dma((chunks, PIECES)),
            dma((PIECES,)),
        ],
        compiler_params=pltpu.CompilerParams(
            collective_id=0, has_side_effects=True, vmem_limit_bytes=60 * 2**20
        ),
        cost_estimate=pl.CostEstimate(
            flops=2 * rows * 16 * half * units * 2, bytes_accessed=2 * (rows * half + 2 * depth * units + rows * units), transcendentals=0
        ),
    )(tokens, gate_weight, up_weight)
    return pl.pallas_call(
        closing,
        out_shape=jax.ShapeDtypeStruct((rows, units), jnp.bfloat16),
        in_specs=[any_space] * 3,
        out_specs=any_space,
        scratch_shapes=[
            pltpu.VMEM((rows, units), jnp.bfloat16),
            pltpu.VMEM((rows, 2 * LANES), jnp.float32),
            pltpu.VMEM((2, rows, LANES), jnp.bfloat16),
            dma((PIECES, 4)),
            dma((PIECES,)),
        ],
    )(*parts)


def solution(mesh):
    placed = (P("row", "col"), P("row", "col"), P("row", "col"))
    return jax.shard_map(
        on_device, mesh=mesh, in_specs=placed, out_specs=P("row", "col"), check_vma=False
    )
```

```python
import functools

import jax
import jax.numpy as jnp
from jax import lax
from jax.experimental import pallas as pl
from jax.experimental.pallas import tpu as pltpu
from jax.sharding import PartitionSpec as P

MESH = pl.DeviceIdType.MESH
LANES = 128
PIECES = 3


def encode(v):
    w = v * 2.0**14
    w2 = w * w
    return (w2 * w2 * w).astype(jnp.bfloat16)


def decode(u):
    u = u.astype(jnp.float32)
    r = jnp.exp2(jnp.log2(jnp.abs(u)) * 0.2 - 14.0)
    return jnp.where(u < 0, -r, r)


def kernel(
    tok, gate, up, hidden, last_own_sums, last_got,
    wb, tb, send, got, acc, ahead, out,
    w_in, w_out, w_local, t_in, t_sib, y_out, x_out, s_out, o_in, o_out, done, kept,
):
    rows, half = tok.shape
    depth, units = gate.shape
    chunks = units // LANES
    piece = rows // PIECES
    last = 2 * chunks - 2
    row, col = lax.axis_index("row"), lax.axis_index("col")
    yh, z = row // 4, row % 4
    x, yl, core = col // 4, (col // 2) % 2, col % 2
    b = x % 2
    source = (x // 2) == yh
    y = yh * 2 + yl

    def at(x=x, y=y, z=z, core=core):
        return ((y // 2) * 4 + z, x * 4 + (y % 2) * 2 + core)

    z_next, z_prev = (z + 1) % 4, (z + 3) % 4
    x_next, x_prev = (x + 1) % 4, (x + 3) % 4
    right, left = at(z=z_next), at(z=z_prev)
    partner = at(y=(y + 2) % 4)
    flip = at(y=yh * 2 + 1 - yl)
    cross = at(y=(1 - yh) * 2 + 1 - yl)
    sibling = at(core=1 - core)
    pair = at(x=jnp.where(b == 0, x_next, x_prev))
    outer = at(x=jnp.where(b == 0, x_prev, x_next))

    def remote(src, dst, ssem, rsem, to):
        return pltpu.make_async_remote_copy(
            src_ref=src, dst_ref=dst, send_sem=ssem, recv_sem=rsem, device_id=to, device_id_type=MESH
        )

    def lines(m, size=piece):
        return pl.ds(pl.multiple_of(m * size, size), size)

    def landed(ref, sem):
        pltpu.make_async_copy(ref, ref, sem).wait()

    def slot(h, s, lo=0, size=depth):
        return wb.at[h, pl.ds(pl.multiple_of(s * depth + lo, size), size), :]

    def pack(n):
        lane = pl.ds(n * LANES, LANES)
        return (
            pltpu.make_async_copy(gate.at[:, lane], slot(2 * n, z), w_local.at[2 * n]),
            pltpu.make_async_copy(up.at[:, lane], slot(2 * n + 1, z), w_local.at[2 * n + 1]),
        )

    def first_half(h):
        top, low = slot(h, z, 0, depth // 2), slot(h, z, depth // 2, depth // 2)
        return (
            remote(top, top, w_out.at[h, 0], w_in.at[h, 0], right),
            remote(low, low, w_out.at[h, 1], w_in.at[h, 1], left),
        )

    def second_half(h):
        top, low = slot(h, z, 0, depth // 2), slot(h, z, depth // 2, depth // 2)
        return (
            remote(low, low, w_out.at[h, 2], w_in.at[h, 2], right),
            remote(top, top, w_out.at[h, 3], w_in.at[h, 3], left),
        )

    def relayed(h):
        top = slot(h, z_prev, 0, depth // 2)
        low = slot(h, z_next, depth // 2, depth // 2)
        return (
            remote(top, top, w_out.at[h, 4], w_in.at[h, 4], right),
            remote(low, low, w_out.at[h, 5], w_in.at[h, 5], left),
        )

    def start_first(h):
        landed(slot(h, z), w_local.at[h])
        for copy in first_half(h):
            copy.start()

    def start_second(h):
        for copy in second_half(h):
            copy.start()

    def weights_step(h):
        first, second = relayed(h)
        landed(slot(h, z_prev, 0, depth // 2), w_in.at[h, 0])
        first.start()
        landed(slot(h, z_next, depth // 2, depth // 2), w_in.at[h, 1])
        second.start()

        @pl.when(h == last)
        def _():
            start_first(h + 1)

        @pl.when(h + 1 < 2 * chunks)
        def _():
            start_second(h + 1)

        @pl.when(h + 2 < 2 * chunks - 1)
        def _():
            start_first(h + 2)

    def weights_ready(h):
        far = (z + 2) % 4
        landed(slot(h, z_prev, depth // 2, depth // 2), w_in.at[h, 2])
        landed(slot(h, z_next, 0, depth // 2), w_in.at[h, 3])
        landed(slot(h, far, 0, depth // 2), w_in.at[h, 4])
        landed(slot(h, far, depth // 2, depth // 2), w_in.at[h, 5])

    def block(r, p, j, c):
        return tb.at[r, p, j, c]

    def tokens_of(r, p):
        return jnp.concatenate([tb[r, p, j, c] for j in range(4) for c in range(2)], axis=1)

    own_j = b * 2 + yl

    def cross_send(p):
        return remote(tok.at[lines(p), :], block(0, p, own_j, core), y_out.at[0, p], t_in.at[0, p, own_j], cross)

    def flip_send(p):
        return remote(tok.at[lines(p), :], block(1, p, own_j, core), y_out.at[1, p], t_in.at[1, p, own_j], flip)

    def flip_pass(p):
        here = block(0, p, b * 2 + 1 - yl, core)
        return remote(here, here, y_out.at[0, p], t_in.at[0, p, b * 2 + 1 - yl], flip)

    def keep(p):
        return pltpu.make_async_copy(tok.at[lines(p), :], block(1, p, own_j, core), t_in.at[1, p, own_j])

    def cross_step(p):
        @pl.when(jnp.logical_not(source))
        def _():
            if p:
                cross_send(p - 1).wait_send()
            cross_send(p).start()

    def flip_step(p):
        @pl.when(source)
        def _():
            flip_send(p).start()

    def near_j(q):
        return b * 2 + (yl + 1 + q) % 2

    def far_j(q):
        return (1 - b) * 2 + (yl + 1 + q) % 2

    def index(r, p, q):
        return (r * PIECES + p) * 2 + q

    def to_sibling(r, p, j, i, g):
        here = block(r, p, j, core)
        return remote(here, here, s_out.at[i, g], t_sib.at[r, p, j], sibling)

    def outward(r, p, j, i, e, to):
        here = block(r, p, j, core)
        return remote(here, here, x_out.at[i, e], t_in.at[r, p, j], to)

    steps = 4 * PIECES

    def near_step(r, p, q):
        i, j = index(r, p, q), near_j(q)

        @pl.when(source)
        def _():
            landed(block(r, p, j, core), t_in.at[r, p, j])
            outward(r, p, j, i, 0, pair).start()
            outward(r, p, j, i, 1, outer).start()
            if isinstance(r, int) and r == 0 and q == 0:
                flip_pass(p).start()
            to_sibling(r, p, j, i, 0).start()

    def far_step(r, p, q):
        i, j = index(r, p, q), far_j(q)
        landed(block(r, p, j, core), t_in.at[r, p, j])

        @pl.when(jnp.logical_not(source))
        def _():
            outward(r, p, j, i, 0, pair).start()

        to_sibling(r, p, j, i, 1).start()

    def last_step(r, p, q):
        i, j = index(r, p, q), near_j(q)

        @pl.when(jnp.logical_not(source))
        def _():
            landed(block(r, p, j, core), t_in.at[r, p, j])
            to_sibling(r, p, j, i, 0).start()

    def own_rows(k):
        return 1, k // 2, 1 - k % 2

    def tokens_ready(r, p):
        for j in range(4):
            landed(block(r, p, j, 1 - core), t_sib.at[r, p, j])

    def partial(h, m):
        return remote(send.at[h, lines(m)], got.at[h, lines(m)], o_out.at[h, m], o_in.at[h, m], partner)

    def last_partial(g, m):
        h = last + g
        return remote(send.at[h, lines(m)], last_got.at[g, lines(m)], o_out.at[h, m], o_in.at[h, m], partner)

    def both(n):
        return jnp.concatenate([wb[2 * n], wb[2 * n + 1]], axis=1)

    def send_pair(n):
        weights_ready(2 * n)
        weights_ready(2 * n + 1)

        @pl.loop(0, PIECES)
        def _(m):
            part = jnp.dot(tokens_of(0, m), both(n), preferred_element_type=jnp.float32)
            for g in range(2):
                send[2 * n + g, lines(m), :] = encode(part[:, g * LANES : (g + 1) * LANES])
                partial(2 * n + g, m).start()

    def send_part(h):
        weights_ready(h)

        @pl.loop(0, PIECES)
        def _(m):
            part = jnp.dot(tokens_of(0, m), wb[h], preferred_element_type=jnp.float32)
            send[h, lines(m), :] = encode(part)

            @pl.when(h < last)
            def _():
                partial(h, m).start()

            @pl.when(h == last)
            def _():
                last_partial(0, m).start()

    def some(m, s):
        rows_of = jnp.concatenate([tb[0, m, s, c] for c in range(2)], axis=1)
        return jnp.dot(rows_of, wb[last + 1, pl.ds(pl.multiple_of(s * depth, depth), depth), :], preferred_element_type=jnp.float32)

    def last_up_ahead():
        landed(slot(last + 1, z_prev, depth // 2, depth // 2), w_in.at[last + 1, 2])
        landed(slot(last + 1, z_next, 0, depth // 2), w_in.at[last + 1, 3])

        @pl.loop(0, PIECES)
        def _(m):
            ahead[lines(m), :] = some(m, z) + some(m, z_prev) + some(m, z_next)

    def last_up():
        far = (z + 2) % 4
        landed(slot(last + 1, far, 0, depth // 2), w_in.at[last + 1, 4])
        landed(slot(last + 1, far, depth // 2, depth // 2), w_in.at[last + 1, 5])

        @pl.loop(0, PIECES)
        def _(m):
            send[last + 1, lines(m), :] = encode(ahead[lines(m), :] + some(m, far))
            last_partial(1, m).start()

    def last_own(g):
        @pl.loop(0, PIECES)
        def _(m):
            acc[lines(m), pl.ds(g * LANES, LANES)] = jnp.dot(tokens_of(1, m), wb[last + g], preferred_element_type=jnp.float32)
            kept_sums(g, m).start()

    def kept_sums(g, m):
        lane = pl.ds(g * LANES, LANES)
        return pltpu.make_async_copy(acc.at[lines(m), lane], last_own_sums.at[lines(m), lane], kept.at[g, m])

    def own_product(n, m):
        acc[lines(m), :] = jnp.dot(tokens_of(1, m), both(n), preferred_element_type=jnp.float32)

    def own_finish(n, m):
        landed(got.at[2 * n, lines(m)], o_in.at[2 * n, m])
        landed(got.at[2 * n + 1, lines(m)], o_in.at[2 * n + 1, m])

        @pl.loop(m * (piece // 32), (m + 1) * (piece // 32))
        def _(t):
            here = lines(t, 32)
            g = acc[here, :LANES] + decode(got[2 * n, here, :])
            u = acc[here, LANES:] + decode(got[2 * n + 1, here, :])
            out[n, here, :] = (g / (1.0 + jnp.exp(-g)) * u).astype(out.dtype)

        result(n, m).start()

    def result(n, m):
        lane = pl.ds(pl.multiple_of(n * LANES, LANES), LANES)
        return pltpu.make_async_copy(out.at[n, lines(m)], hidden.at[lines(m), lane], done.at[n, m])

    barrier = pltpu.get_barrier_semaphore()
    neighbours = (right, left, partner, flip, cross, sibling, pair, outer)
    for to in neighbours:
        pl.semaphore_signal(barrier, inc=1, device_id=to, device_id_type=MESH)
    for n in range(chunks):
        for copy in pack(n):
            copy.start()
    pl.semaphore_wait(barrier, len(neighbours))

    start_first(0)
    start_second(0)
    cross_step(0)

    @pl.when(source)
    def _():
        for p in range(PIECES):
            keep(p).start()

    start_first(1)

    early = (
        ((cross_step, 1), (near_step, 0, 0, 0), (cross_step, 2), (near_step, 0, 1, 0)),
        ((near_step, 0, 0, 1), (far_step, 0, 0, 0), (near_step, 0, 2, 0), (near_step, 0, 1, 1), (far_step, 0, 1, 0), (last_step, 0, 0, 0)),
        ((near_step, 0, 2, 1), (far_step, 0, 0, 1), (last_step, 0, 1, 0), (flip_step, 0)),
        ((near_step, *own_rows(0)), (far_step, 0, 2, 0), (last_step, 0, 0, 1), (flip_step, 1), (far_step, 0, 1, 1), (last_step, 0, 2, 0), (flip_step, 2)),
        ((near_step, *own_rows(1)), (near_step, *own_rows(2)), (far_step, 0, 2, 1), (last_step, 0, 1, 1)),
        ((last_step, 0, 2, 1), *((near_step, *own_rows(k)) for k in (3, 4, 5)), (far_step, *own_rows(0))),
    )
    for h, events in enumerate(early):
        weights_step(h)
        for event, *which in events:
            event(*which)
    for p in range(PIECES):
        tokens_ready(0, p)
    late = len(early)

    def unit(k):
        return jnp.where(k < 9, k % 3, 3 + (k - 9) // 3), jnp.where(k < 9, k // 3, (k - 9) % 3)

    def steps_at(h, counts):
        done = [jnp.int32(0)] + [jnp.int32(c) for c in counts]
        lo, hi = done[0], done[1]
        for i in range(1, len(counts)):
            lo = jnp.where(h >= late + i, done[i], lo)
            hi = jnp.where(h >= late + i, done[i + 1], hi)
        return lo, hi

    @pl.loop(late, last + 2)
    def _(h):
        weights_step(h)

        @pl.loop(*steps_at(h, (1, 3, 4, 5, 5, 5, 5, 5)))
        def _(k):
            far_step(*own_rows(k + 1))

        @pl.loop(*steps_at(h, (1, 2, 4, 5, 6, 6, 6, 6)))
        def _(k):
            last_step(*own_rows(k))

        @pl.loop(*steps_at(h, (2, 3, 4, 4, 5, 5, 5, 5)))
        def _(n):
            send_pair(n)

        @pl.loop(*steps_at(h, (10, 10, 10, 10, 10, 11, 12, 13)))
        def _(k):
            @pl.when(k >= 10)
            def _():
                send_part(k)

        @pl.when(jnp.logical_and(h >= 8, h <= 10))
        def _():
            tokens_ready(1, h - 8)

        @pl.loop(*steps_at(h, (0, 0, 2, 6, 10, 12, 18, 18)))
        def _(k):
            n, m = unit(k)
            own_product(n, m)

            @pl.when(k < 15)
            def _():
                own_finish(n, m)

    @pl.loop(0, PIECES)
    def _(m):
        own_finish(chunks - 2, m)

    last_up_ahead()
    last_up()
    last_own(0)
    last_own(1)

    @pl.loop(0, 2 * chunks)
    def _(h):
        for copy in first_half(h) + second_half(h) + relayed(h):
            copy.wait_send()

        @pl.when(h < last)
        def _():
            @pl.loop(0, PIECES)
            def _(m):
                partial(h, m).wait_send()

    @pl.loop(0, chunks - 1)
    def _(n):
        @pl.loop(0, PIECES)
        def _(m):
            result(n, m).wait()

    for p in range(PIECES):
        @pl.when(source)
        def _():
            flip_pass(p).wait_send()
            flip_send(p).wait_send()

    @pl.when(jnp.logical_not(source))
    def _():
        cross_send(PIECES - 1).wait_send()

    @pl.loop(0, steps)
    def _(i):
        r, p, j = i // (2 * PIECES), (i // 2) % PIECES, b * 2
        outward(r, p, j, i, 0, pair).wait_send()
        to_sibling(r, p, j, i, 0).wait_send()
        to_sibling(r, p, j, i, 1).wait_send()

        @pl.when(source)
        def _():
            outward(r, p, j, i, 1, outer).wait_send()

    for m in range(PIECES):
        for g in range(2):
            kept_sums(g, m).wait()
            last_partial(g, m).wait_send()
            landed(last_got.at[g, lines(m)], o_in.at[last + g, m])


def closing(hidden, last_own, last_got, out, whole, own, got, sem_in, sem_out):
    rows, units = out.shape
    piece = rows // PIECES
    known = units - LANES

    def lines(m):
        return pl.ds(m * piece, piece)

    def loads(m):
        return (
            pltpu.make_async_copy(last_own.at[lines(m)], own.at[lines(m)], sem_in.at[m, 0]),
            pltpu.make_async_copy(last_got.at[0, lines(m)], got.at[0, lines(m)], sem_in.at[m, 1]),
            pltpu.make_async_copy(last_got.at[1, lines(m)], got.at[1, lines(m)], sem_in.at[m, 2]),
            pltpu.make_async_copy(hidden.at[lines(m)], whole.at[lines(m), pl.ds(0, known)], sem_in.at[m, 3]),
        )

    def store(m):
        return pltpu.make_async_copy(whole.at[lines(m)], out.at[lines(m)], sem_out.at[m])

    for m in range(PIECES):
        for copy in loads(m):
            copy.start()
    for m in range(PIECES):
        for copy in loads(m):
            copy.wait()

        @pl.loop(m * (piece // 32), (m + 1) * (piece // 32))
        def _(t):
            here = pl.ds(pl.multiple_of(t * 32, 32), 32)
            g = own[here, :LANES] + decode(got[0, here, :])
            u = own[here, LANES:] + decode(got[1, here, :])
            whole[here, pl.ds(known, LANES)] = (g / (1.0 + jnp.exp(-g)) * u).astype(out.dtype)

        store(m).start()
    for m in range(PIECES):
        store(m).wait()


def on_device(tokens, gate_weight, up_weight):
    rows, half = tokens.shape
    depth, units = gate_weight.shape
    chunks = units // LANES
    dma = pltpu.SemaphoreType.DMA
    any_space = pl.BlockSpec(memory_space=pl.ANY)
    parts = pl.pallas_call(
        kernel,
        out_shape=(
            jax.ShapeDtypeStruct((rows, units - LANES), jnp.bfloat16),
            jax.ShapeDtypeStruct((rows, 2 * LANES), jnp.float32),
            jax.ShapeDtypeStruct((2, rows, LANES), jnp.bfloat16),
        ),
        in_specs=[any_space] * 3,
        out_specs=(any_space,) * 3,
        scratch_shapes=[
            pltpu.VMEM((2 * chunks, 4 * depth, LANES), jnp.bfloat16),
            pltpu.VMEM((2, PIECES, 4, 2, rows // PIECES, half), jnp.bfloat16),
            pltpu.VMEM((2 * chunks, rows, LANES), jnp.bfloat16),
            pltpu.VMEM((2 * chunks, rows, LANES), jnp.bfloat16),
            pltpu.VMEM((rows, 2 * LANES), jnp.float32),
            pltpu.VMEM((rows, LANES), jnp.float32),
            pltpu.VMEM((chunks, rows, LANES), jnp.bfloat16),
            dma((2 * chunks, 6)),
            dma((2 * chunks, 6)),
            dma((2 * chunks,)),
            dma((2, PIECES, 4)),
            dma((2, PIECES, 4)),
            dma((2, PIECES)),
            dma((4 * PIECES, 2)),
            dma((4 * PIECES, 2)),
            dma((2 * chunks, PIECES)),
            dma((2 * chunks, PIECES)),
            dma((chunks, PIECES)),
            dma((2, PIECES)),
        ],
        compiler_params=pltpu.CompilerParams(
            collective_id=0, has_side_effects=True, vmem_limit_bytes=60 * 2**20
        ),
        cost_estimate=pl.CostEstimate(
            flops=2 * rows * 16 * half * units * 2, bytes_accessed=2 * (rows * half + 2 * depth * units + rows * units), transcendentals=0
        ),
    )(tokens, gate_weight, up_weight)
    return pl.pallas_call(
        closing,
        out_shape=jax.ShapeDtypeStruct((rows, units), jnp.bfloat16),
        in_specs=[any_space] * 3,
        out_specs=any_space,
        scratch_shapes=[
            pltpu.VMEM((rows, units), jnp.bfloat16),
            pltpu.VMEM((rows, 2 * LANES), jnp.float32),
            pltpu.VMEM((2, rows, LANES), jnp.bfloat16),
            dma((PIECES, 4)),
            dma((PIECES,)),
        ],
    )(*parts)


def solution(mesh):
    placed = (P("row", "col"), P("row", "col"), P("row", "col"))
    return jax.shard_map(
        on_device, mesh=mesh, in_specs=placed, out_specs=P("row", "col"), check_vma=False
    )
```

```python
import functools

import jax
import jax.numpy as jnp
from jax import lax
from jax.experimental import pallas as pl
from jax.experimental.pallas import tpu as pltpu
from jax.sharding import PartitionSpec as P

MESH = pl.DeviceIdType.MESH
LANES = 128
PIECES = 3


def encode(v):
    w = v * 2.0**14
    w2 = w * w
    return (w2 * w2 * w).astype(jnp.bfloat16)


def decode(u):
    u = u.astype(jnp.float32)
    r = jnp.exp2(jnp.log2(jnp.abs(u)) * 0.2 - 14.0)
    return jnp.where(u < 0, -r, r)


def kernel(
    tok, gate, up, hidden, last_own_sums, last_got,
    wb, tb, send, got, acc, ahead, out,
    w_in, w_out, w_local, t_in, t_sib, y_out, x_out, s_out, o_in, o_out, done, kept,
):
    rows, half = tok.shape
    depth, units = gate.shape
    chunks = units // LANES
    piece = rows // PIECES
    last = 2 * chunks - 2
    row, col = lax.axis_index("row"), lax.axis_index("col")
    yh, z = row // 4, row % 4
    x, yl, core = col // 4, (col // 2) % 2, col % 2
    b = x % 2
    source = (x // 2) == yh
    y = yh * 2 + yl

    def at(x=x, y=y, z=z, core=core):
        return ((y // 2) * 4 + z, x * 4 + (y % 2) * 2 + core)

    z_next, z_prev = (z + 1) % 4, (z + 3) % 4
    x_next, x_prev = (x + 1) % 4, (x + 3) % 4
    right, left = at(z=z_next), at(z=z_prev)
    partner = at(y=(y + 2) % 4)
    flip = at(y=yh * 2 + 1 - yl)
    cross = at(y=(1 - yh) * 2 + 1 - yl)
    sibling = at(core=1 - core)
    pair = at(x=jnp.where(b == 0, x_next, x_prev))
    outer = at(x=jnp.where(b == 0, x_prev, x_next))

    def remote(src, dst, ssem, rsem, to):
        return pltpu.make_async_remote_copy(
            src_ref=src, dst_ref=dst, send_sem=ssem, recv_sem=rsem, device_id=to, device_id_type=MESH
        )

    def lines(m, size=piece):
        return pl.ds(pl.multiple_of(m * size, size), size)

    def landed(ref, sem):
        pltpu.make_async_copy(ref, ref, sem).wait()

    def slot(h, s, lo=0, size=depth):
        return wb.at[h, pl.ds(pl.multiple_of(s * depth + lo, size), size), :]

    def pack(n):
        lane = pl.ds(n * LANES, LANES)
        return (
            pltpu.make_async_copy(gate.at[:, lane], slot(2 * n, z), w_local.at[2 * n]),
            pltpu.make_async_copy(up.at[:, lane], slot(2 * n + 1, z), w_local.at[2 * n + 1]),
        )

    def first_half(h):
        top, low = slot(h, z, 0, depth // 2), slot(h, z, depth // 2, depth // 2)
        return (
            remote(top, top, w_out.at[h, 0], w_in.at[h, 0], right),
            remote(low, low, w_out.at[h, 1], w_in.at[h, 1], left),
        )

    def second_half(h):
        top, low = slot(h, z, 0, depth // 2), slot(h, z, depth // 2, depth // 2)
        return (
            remote(low, low, w_out.at[h, 2], w_in.at[h, 2], right),
            remote(top, top, w_out.at[h, 3], w_in.at[h, 3], left),
        )

    def relayed(h):
        top = slot(h, z_prev, 0, depth // 2)
        low = slot(h, z_next, depth // 2, depth // 2)
        return (
            remote(top, top, w_out.at[h, 4], w_in.at[h, 4], right),
            remote(low, low, w_out.at[h, 5], w_in.at[h, 5], left),
        )

    def start_first(h):
        landed(slot(h, z), w_local.at[h])
        for copy in first_half(h):
            copy.start()

    def start_second(h):
        for copy in second_half(h):
            copy.start()

    def weights_step(h):
        first, second = relayed(h)
        landed(slot(h, z_prev, 0, depth // 2), w_in.at[h, 0])
        first.start()
        landed(slot(h, z_next, depth // 2, depth // 2), w_in.at[h, 1])
        second.start()

        @pl.when(h == last)
        def _():
            start_first(h + 1)

        @pl.when(h + 1 < 2 * chunks)
        def _():
            start_second(h + 1)

        @pl.when(h + 2 < 2 * chunks - 1)
        def _():
            start_first(h + 2)

    def weights_ready(h):
        far = (z + 2) % 4
        landed(slot(h, z_prev, depth // 2, depth // 2), w_in.at[h, 2])
        landed(slot(h, z_next, 0, depth // 2), w_in.at[h, 3])
        landed(slot(h, far, 0, depth // 2), w_in.at[h, 4])
        landed(slot(h, far, depth // 2, depth // 2), w_in.at[h, 5])

    def block(r, p, j, c):
        return tb.at[r, p, j, c]

    def tokens_of(r, p):
        return jnp.concatenate([tb[r, p, j, c] for j in range(4) for c in range(2)], axis=1)

    own_j = b * 2 + yl

    def cross_send(p):
        return remote(tok.at[lines(p), :], block(0, p, own_j, core), y_out.at[0, p], t_in.at[0, p, own_j], cross)

    def flip_send(p):
        return remote(tok.at[lines(p), :], block(1, p, own_j, core), y_out.at[1, p], t_in.at[1, p, own_j], flip)

    def flip_pass(p):
        here = block(0, p, b * 2 + 1 - yl, core)
        return remote(here, here, y_out.at[0, p], t_in.at[0, p, b * 2 + 1 - yl], flip)

    def keep(p):
        return pltpu.make_async_copy(tok.at[lines(p), :], block(1, p, own_j, core), t_in.at[1, p, own_j])

    def cross_step(p):
        @pl.when(jnp.logical_not(source))
        def _():
            if p:
                cross_send(p - 1).wait_send()
            cross_send(p).start()

    def flip_step(p):
        @pl.when(source)
        def _():
            flip_send(p).start()

    def near_j(q):
        return b * 2 + (yl + 1 + q) % 2

    def far_j(q):
        return (1 - b) * 2 + (yl + 1 + q) % 2

    def index(r, p, q):
        return (r * PIECES + p) * 2 + q

    def to_sibling(r, p, j, i, g):
        here = block(r, p, j, core)
        return remote(here, here, s_out.at[i, g], t_sib.at[r, p, j], sibling)

    def outward(r, p, j, i, e, to):
        here = block(r, p, j, core)
        return remote(here, here, x_out.at[i, e], t_in.at[r, p, j], to)

    steps = 4 * PIECES

    def near_step(r, p, q):
        i, j = index(r, p, q), near_j(q)

        @pl.when(source)
        def _():
            landed(block(r, p, j, core), t_in.at[r, p, j])
            outward(r, p, j, i, 0, pair).start()
            outward(r, p, j, i, 1, outer).start()
            if isinstance(r, int) and r == 0 and q == 0:
                flip_pass(p).start()
            to_sibling(r, p, j, i, 0).start()

    def far_step(r, p, q):
        i, j = index(r, p, q), far_j(q)
        landed(block(r, p, j, core), t_in.at[r, p, j])

        @pl.when(jnp.logical_not(source))
        def _():
            outward(r, p, j, i, 0, pair).start()

        to_sibling(r, p, j, i, 1).start()

    def last_step(r, p, q):
        i, j = index(r, p, q), near_j(q)

        @pl.when(jnp.logical_not(source))
        def _():
            landed(block(r, p, j, core), t_in.at[r, p, j])
            to_sibling(r, p, j, i, 0).start()

    def own_rows(k):
        return 1, k // 2, 1 - k % 2

    def tokens_ready(r, p):
        for j in range(4):
            landed(block(r, p, j, 1 - core), t_sib.at[r, p, j])

    def partial(h, m):
        return remote(send.at[h, lines(m)], got.at[h, lines(m)], o_out.at[h, m], o_in.at[h, m], partner)

    def last_partial(g, m):
        h = last + g
        return remote(send.at[h, lines(m)], last_got.at[g, lines(m)], o_out.at[h, m], o_in.at[h, m], partner)

    def both(n):
        return jnp.concatenate([wb[2 * n], wb[2 * n + 1]], axis=1)

    def send_pair(n):
        weights_ready(2 * n)
        weights_ready(2 * n + 1)

        @pl.loop(0, PIECES)
        def _(m):
            part = jnp.dot(tokens_of(0, m), both(n), preferred_element_type=jnp.float32)
            for g in range(2):
                send[2 * n + g, lines(m), :] = encode(part[:, g * LANES : (g + 1) * LANES])
                partial(2 * n + g, m).start()

    def send_part(h):
        weights_ready(h)

        @pl.loop(0, PIECES)
        def _(m):
            part = jnp.dot(tokens_of(0, m), wb[h], preferred_element_type=jnp.float32)
            send[h, lines(m), :] = encode(part)

            @pl.when(h < last)
            def _():
                partial(h, m).start()

            @pl.when(h == last)
            def _():
                last_partial(0, m).start()

    def some(m, s):
        rows_of = jnp.concatenate([tb[0, m, s, c] for c in range(2)], axis=1)
        return jnp.dot(rows_of, wb[last + 1, pl.ds(pl.multiple_of(s * depth, depth), depth), :], preferred_element_type=jnp.float32)

    def last_up_ahead():
        landed(slot(last + 1, z_prev, depth // 2, depth // 2), w_in.at[last + 1, 2])
        landed(slot(last + 1, z_next, 0, depth // 2), w_in.at[last + 1, 3])

        @pl.loop(0, PIECES)
        def _(m):
            ahead[lines(m), :] = some(m, z) + some(m, z_prev) + some(m, z_next)

    def last_up():
        far = (z + 2) % 4
        landed(slot(last + 1, far, 0, depth // 2), w_in.at[last + 1, 4])
        landed(slot(last + 1, far, depth // 2, depth // 2), w_in.at[last + 1, 5])

        @pl.loop(0, PIECES)
        def _(m):
            send[last + 1, lines(m), :] = encode(ahead[lines(m), :] + some(m, far))
            last_partial(1, m).start()

    def last_own(g):
        @pl.loop(0, PIECES)
        def _(m):
            acc[lines(m), pl.ds(g * LANES, LANES)] = jnp.dot(tokens_of(1, m), wb[last + g], preferred_element_type=jnp.float32)
            kept_sums(g, m).start()

    def kept_sums(g, m):
        lane = pl.ds(g * LANES, LANES)
        return pltpu.make_async_copy(acc.at[lines(m), lane], last_own_sums.at[lines(m), lane], kept.at[g, m])

    def own_product(n, m):
        acc[lines(m), :] = jnp.dot(tokens_of(1, m), both(n), preferred_element_type=jnp.float32)

    def own_finish(n, m):
        landed(got.at[2 * n, lines(m)], o_in.at[2 * n, m])
        landed(got.at[2 * n + 1, lines(m)], o_in.at[2 * n + 1, m])

        @pl.loop(m * (piece // 32), (m + 1) * (piece // 32))
        def _(t):
            here = lines(t, 32)
            g = acc[here, :LANES] + decode(got[2 * n, here, :])
            u = acc[here, LANES:] + decode(got[2 * n + 1, here, :])
            out[n, here, :] = (g / (1.0 + jnp.exp(-g)) * u).astype(out.dtype)

        result(n, m).start()

    def result(n, m):
        lane = pl.ds(pl.multiple_of(n * LANES, LANES), LANES)
        return pltpu.make_async_copy(out.at[n, lines(m)], hidden.at[lines(m), lane], done.at[n, m])

    sent_early = 8

    def weights_sent(h):
        for copy in first_half(h) + second_half(h) + relayed(h):
            copy.wait_send()

    def partial_sent(h):
        @pl.loop(0, PIECES)
        def _(m):
            partial(h, m).wait_send()

    def tokens_sent():
        for p in range(PIECES):
            @pl.when(source)
            def _():
                flip_pass(p).wait_send()
                flip_send(p).wait_send()

        @pl.when(jnp.logical_not(source))
        def _():
            cross_send(PIECES - 1).wait_send()

        @pl.loop(0, steps)
        def _(i):
            r, p, j = i // (2 * PIECES), (i // 2) % PIECES, b * 2
            outward(r, p, j, i, 0, pair).wait_send()
            to_sibling(r, p, j, i, 0).wait_send()
            to_sibling(r, p, j, i, 1).wait_send()

            @pl.when(source)
            def _():
                outward(r, p, j, i, 1, outer).wait_send()

    barrier = pltpu.get_barrier_semaphore()
    neighbours = (right, left, partner, flip, cross, sibling, pair, outer)
    for to in neighbours:
        pl.semaphore_signal(barrier, inc=1, device_id=to, device_id_type=MESH)
    for n in range(chunks):
        for copy in pack(n):
            copy.start()
    pl.semaphore_wait(barrier, len(neighbours))

    start_first(0)
    start_second(0)
    cross_step(0)

    @pl.when(source)
    def _():
        for p in range(PIECES):
            keep(p).start()

    start_first(1)

    early = (
        ((cross_step, 1), (near_step, 0, 0, 0), (cross_step, 2), (near_step, 0, 1, 0)),
        ((near_step, 0, 0, 1), (far_step, 0, 0, 0), (near_step, 0, 2, 0), (near_step, 0, 1, 1), (far_step, 0, 1, 0), (last_step, 0, 0, 0)),
        ((near_step, 0, 2, 1), (far_step, 0, 0, 1), (last_step, 0, 1, 0), (flip_step, 0)),
        ((near_step, *own_rows(0)), (far_step, 0, 2, 0), (last_step, 0, 0, 1), (flip_step, 1), (far_step, 0, 1, 1), (last_step, 0, 2, 0), (flip_step, 2)),
        ((near_step, *own_rows(1)), (near_step, *own_rows(2)), (far_step, 0, 2, 1), (last_step, 0, 1, 1)),
        ((last_step, 0, 2, 1), *((near_step, *own_rows(k)) for k in (3, 4, 5)), (far_step, *own_rows(0))),
    )
    for h, events in enumerate(early):
        weights_step(h)
        for event, *which in events:
            event(*which)
    for p in range(PIECES):
        tokens_ready(0, p)
    late = len(early)

    def unit(k):
        return jnp.where(k < 9, k % 3, 3 + (k - 9) // 3), jnp.where(k < 9, k // 3, (k - 9) % 3)

    def steps_at(h, counts):
        done = [jnp.int32(0)] + [jnp.int32(c) for c in counts]
        lo, hi = done[0], done[1]
        for i in range(1, len(counts)):
            lo = jnp.where(h >= late + i, done[i], lo)
            hi = jnp.where(h >= late + i, done[i + 1], hi)
        return lo, hi

    @pl.loop(late, last + 2)
    def _(h):
        weights_step(h)

        @pl.loop(*steps_at(h, (1, 3, 4, 5, 5, 5, 5, 5)))
        def _(k):
            far_step(*own_rows(k + 1))

        @pl.loop(*steps_at(h, (1, 2, 4, 5, 6, 6, 6, 6)))
        def _(k):
            last_step(*own_rows(k))

        @pl.loop(*steps_at(h, (2, 3, 4, 4, 5, 5, 5, 5)))
        def _(n):
            send_pair(n)

        @pl.loop(*steps_at(h, (10, 10, 10, 10, 10, 11, 12, 13)))
        def _(k):
            @pl.when(k >= 10)
            def _():
                send_part(k)

        @pl.when(jnp.logical_and(h >= 8, h <= 10))
        def _():
            tokens_ready(1, h - 8)

        @pl.loop(*steps_at(h, (0, 0, 2, 6, 10, 12, 18, 18)))
        def _(k):
            n, m = unit(k)
            own_product(n, m)

            @pl.when(k < 15)
            def _():
                own_finish(n, m)

        weights_sent(h - late)

        @pl.when(h == 11)
        def _():
            tokens_sent()

        @pl.when(h == last + 1)
        def _():
            @pl.loop(0, sent_early)
            def _(k):
                partial_sent(k)

    @pl.loop(0, PIECES)
    def _(m):
        own_finish(chunks - 2, m)

    last_up_ahead()
    last_up()
    last_own(0)
    last_own(1)

    @pl.loop(sent_early, 2 * chunks)
    def _(h):
        weights_sent(h)

        @pl.when(h < last)
        def _():
            partial_sent(h)

    @pl.loop(0, chunks - 1)
    def _(n):
        @pl.loop(0, PIECES)
        def _(m):
            result(n, m).wait()

    for m in range(PIECES):
        for g in range(2):
            kept_sums(g, m).wait()
            last_partial(g, m).wait_send()
            landed(last_got.at[g, lines(m)], o_in.at[last + g, m])


def closing(hidden, last_own, last_got, out, whole, own, got, sem_in, sem_out):
    rows, units = out.shape
    piece = rows // PIECES
    known = units - LANES

    def lines(m):
        return pl.ds(m * piece, piece)

    def loads(m):
        return (
            pltpu.make_async_copy(last_own.at[lines(m)], own.at[lines(m)], sem_in.at[m, 0]),
            pltpu.make_async_copy(last_got.at[0, lines(m)], got.at[0, lines(m)], sem_in.at[m, 1]),
            pltpu.make_async_copy(last_got.at[1, lines(m)], got.at[1, lines(m)], sem_in.at[m, 2]),
        )

    def load_known(m):
        return pltpu.make_async_copy(hidden.at[lines(m)], whole.at[lines(m), pl.ds(0, known)], sem_in.at[m, 3])

    def store(m, i):
        lane = pl.ds(known, LANES) if i else pl.ds(0, known)
        return pltpu.make_async_copy(whole.at[lines(m), lane], out.at[lines(m), lane], sem_out.at[m, i])

    for m in range(PIECES):
        for copy in loads(m):
            copy.start()
    for m in range(PIECES):
        load_known(m).start()
    for m in range(PIECES):
        for copy in loads(m):
            copy.wait()

        @pl.loop(m * (piece // 32), (m + 1) * (piece // 32))
        def _(t):
            here = pl.ds(pl.multiple_of(t * 32, 32), 32)
            g = own[here, :LANES] + decode(got[0, here, :])
            u = own[here, LANES:] + decode(got[1, here, :])
            whole[here, pl.ds(known, LANES)] = (g / (1.0 + jnp.exp(-g)) * u).astype(out.dtype)

        store(m, 1).start()
        load_known(m).wait()
        store(m, 0).start()
    for m in range(PIECES):
        for i in range(2):
            store(m, i).wait()


def on_device(tokens, gate_weight, up_weight):
    rows, half = tokens.shape
    depth, units = gate_weight.shape
    chunks = units // LANES
    dma = pltpu.SemaphoreType.DMA
    any_space = pl.BlockSpec(memory_space=pl.ANY)
    parts = pl.pallas_call(
        kernel,
        out_shape=(
            jax.ShapeDtypeStruct((rows, units - LANES), jnp.bfloat16),
            jax.ShapeDtypeStruct((rows, 2 * LANES), jnp.float32),
            jax.ShapeDtypeStruct((2, rows, LANES), jnp.bfloat16),
        ),
        in_specs=[any_space] * 3,
        out_specs=(any_space,) * 3,
        scratch_shapes=[
            pltpu.VMEM((2 * chunks, 4 * depth, LANES), jnp.bfloat16),
            pltpu.VMEM((2, PIECES, 4, 2, rows // PIECES, half), jnp.bfloat16),
            pltpu.VMEM((2 * chunks, rows, LANES), jnp.bfloat16),
            pltpu.VMEM((2 * chunks, rows, LANES), jnp.bfloat16),
            pltpu.VMEM((rows, 2 * LANES), jnp.float32),
            pltpu.VMEM((rows, LANES), jnp.float32),
            pltpu.VMEM((chunks, rows, LANES), jnp.bfloat16),
            dma((2 * chunks, 6)),
            dma((2 * chunks, 6)),
            dma((2 * chunks,)),
            dma((2, PIECES, 4)),
            dma((2, PIECES, 4)),
            dma((2, PIECES)),
            dma((4 * PIECES, 2)),
            dma((4 * PIECES, 2)),
            dma((2 * chunks, PIECES)),
            dma((2 * chunks, PIECES)),
            dma((chunks, PIECES)),
            dma((2, PIECES)),
        ],
        compiler_params=pltpu.CompilerParams(
            collective_id=0, has_side_effects=True, vmem_limit_bytes=60 * 2**20
        ),
        cost_estimate=pl.CostEstimate(
            flops=2 * rows * 16 * half * units * 2, bytes_accessed=2 * (rows * half + 2 * depth * units + rows * units), transcendentals=0
        ),
    )(tokens, gate_weight, up_weight)
    return pl.pallas_call(
        closing,
        out_shape=jax.ShapeDtypeStruct((rows, units), jnp.bfloat16),
        in_specs=[any_space] * 3,
        out_specs=any_space,
        scratch_shapes=[
            pltpu.VMEM((rows, units), jnp.bfloat16),
            pltpu.VMEM((rows, 2 * LANES), jnp.float32),
            pltpu.VMEM((2, rows, LANES), jnp.bfloat16),
            dma((PIECES, 4)),
            dma((PIECES, 2)),
        ],
    )(*parts)


def solution(mesh):
    placed = (P("row", "col"), P("row", "col"), P("row", "col"))
    return jax.shard_map(
        on_device, mesh=mesh, in_specs=placed, out_specs=P("row", "col"), check_vma=False
    )
```

```python
import functools

import jax
import jax.numpy as jnp
from jax import lax
from jax.experimental import pallas as pl
from jax.experimental.pallas import tpu as pltpu
from jax.sharding import PartitionSpec as P

MESH = pl.DeviceIdType.MESH
LANES = 128
PIECES = 3


def encode(v):
    w = v * 2.0**14
    w2 = w * w
    return (w2 * w2 * w).astype(jnp.bfloat16)


def decode(u):
    u = u.astype(jnp.float32)
    r = jnp.exp2(jnp.log2(jnp.abs(u)) * 0.2 - 14.0)
    return jnp.where(u < 0, -r, r)


def kernel(
    tok, gate, up, hidden, last_own_sums, last_got,
    wb, tb, send, got, acc, ahead, out,
    w_in, w_out, w_local, t_in, t_sib, y_out, x_out, s_out, o_in, o_out, done, kept,
):
    rows, half = tok.shape
    depth, units = gate.shape
    chunks = units // LANES
    piece = rows // PIECES
    last = 2 * chunks - 2
    row, col = lax.axis_index("row"), lax.axis_index("col")
    yh, z = row // 4, row % 4
    x, yl, core = col // 4, (col // 2) % 2, col % 2
    b = x % 2
    source = (x // 2) == yh
    y = yh * 2 + yl

    def at(x=x, y=y, z=z, core=core):
        return ((y // 2) * 4 + z, x * 4 + (y % 2) * 2 + core)

    z_next, z_prev = (z + 1) % 4, (z + 3) % 4
    x_next, x_prev = (x + 1) % 4, (x + 3) % 4
    right, left = at(z=z_next), at(z=z_prev)
    partner = at(y=(y + 2) % 4)
    flip = at(y=yh * 2 + 1 - yl)
    cross = at(y=(1 - yh) * 2 + 1 - yl)
    sibling = at(core=1 - core)
    pair = at(x=jnp.where(b == 0, x_next, x_prev))
    outer = at(x=jnp.where(b == 0, x_prev, x_next))

    def remote(src, dst, ssem, rsem, to):
        return pltpu.make_async_remote_copy(
            src_ref=src, dst_ref=dst, send_sem=ssem, recv_sem=rsem, device_id=to, device_id_type=MESH
        )

    def lines(m, size=piece):
        return pl.ds(pl.multiple_of(m * size, size), size)

    def landed(ref, sem):
        pltpu.make_async_copy(ref, ref, sem).wait()

    def slot(h, s, lo=0, size=depth):
        return wb.at[h, pl.ds(pl.multiple_of(s * depth + lo, size), size), :]

    def pack(n):
        lane = pl.ds(n * LANES, LANES)
        return (
            pltpu.make_async_copy(gate.at[:, lane], slot(2 * n, z), w_local.at[2 * n]),
            pltpu.make_async_copy(up.at[:, lane], slot(2 * n + 1, z), w_local.at[2 * n + 1]),
        )

    def first_half(h):
        top, low = slot(h, z, 0, depth // 2), slot(h, z, depth // 2, depth // 2)
        return (
            remote(top, top, w_out.at[h, 0], w_in.at[h, 0], right),
            remote(low, low, w_out.at[h, 1], w_in.at[h, 1], left),
        )

    def second_half(h):
        top, low = slot(h, z, 0, depth // 2), slot(h, z, depth // 2, depth // 2)
        return (
            remote(low, low, w_out.at[h, 2], w_in.at[h, 2], right),
            remote(top, top, w_out.at[h, 3], w_in.at[h, 3], left),
        )

    def relayed(h):
        top = slot(h, z_prev, 0, depth // 2)
        low = slot(h, z_next, depth // 2, depth // 2)
        return (
            remote(top, top, w_out.at[h, 4], w_in.at[h, 4], right),
            remote(low, low, w_out.at[h, 5], w_in.at[h, 5], left),
        )

    def start_first(h):
        landed(slot(h, z), w_local.at[h])
        for copy in first_half(h):
            copy.start()

    def start_second(h):
        for copy in second_half(h):
            copy.start()

    def weights_step(h):
        first, second = relayed(h)
        landed(slot(h, z_prev, 0, depth // 2), w_in.at[h, 0])
        first.start()
        landed(slot(h, z_next, depth // 2, depth // 2), w_in.at[h, 1])
        second.start()

        @pl.when(h == last)
        def _():
            start_first(h + 1)

        @pl.when(h + 1 < 2 * chunks)
        def _():
            start_second(h + 1)

        @pl.when(h + 2 < 2 * chunks - 1)
        def _():
            start_first(h + 2)

    def weights_ready(h):
        far = (z + 2) % 4
        landed(slot(h, z_prev, depth // 2, depth // 2), w_in.at[h, 2])
        landed(slot(h, z_next, 0, depth // 2), w_in.at[h, 3])
        landed(slot(h, far, 0, depth // 2), w_in.at[h, 4])
        landed(slot(h, far, depth // 2, depth // 2), w_in.at[h, 5])

    def block(r, p, j, c):
        return tb.at[r, p, j, c]

    def tokens_of(r, p):
        return jnp.concatenate([tb[r, p, j, c] for j in range(4) for c in range(2)], axis=1)

    own_j = b * 2 + yl

    def cross_send(p):
        return remote(tok.at[lines(p), :], block(0, p, own_j, core), y_out.at[0, p], t_in.at[0, p, own_j], cross)

    def flip_send(p):
        return remote(tok.at[lines(p), :], block(1, p, own_j, core), y_out.at[1, p], t_in.at[1, p, own_j], flip)

    def flip_pass(p):
        here = block(0, p, b * 2 + 1 - yl, core)
        return remote(here, here, y_out.at[0, p], t_in.at[0, p, b * 2 + 1 - yl], flip)

    def keep(p):
        return pltpu.make_async_copy(tok.at[lines(p), :], block(1, p, own_j, core), t_in.at[1, p, own_j])

    def cross_step(p):
        @pl.when(jnp.logical_not(source))
        def _():
            cross_send(p).start()

    def flip_step(p):
        @pl.when(source)
        def _():
            flip_send(p).start()

    def near_j(q):
        return b * 2 + (yl + 1 + q) % 2

    def far_j(q):
        return (1 - b) * 2 + (yl + 1 + q) % 2

    def index(r, p, q):
        return (r * PIECES + p) * 2 + q

    def to_sibling(r, p, j, i, g):
        here = block(r, p, j, core)
        return remote(here, here, s_out.at[i, g], t_sib.at[r, p, j], sibling)

    def outward(r, p, j, i, e, to):
        here = block(r, p, j, core)
        return remote(here, here, x_out.at[i, e], t_in.at[r, p, j], to)

    steps = 4 * PIECES

    def near_step(r, p, q):
        i, j = index(r, p, q), near_j(q)

        @pl.when(source)
        def _():
            landed(block(r, p, j, core), t_in.at[r, p, j])
            outward(r, p, j, i, 0, pair).start()
            outward(r, p, j, i, 1, outer).start()
            if isinstance(r, int) and r == 0 and q == 0:
                flip_pass(p).start()
            to_sibling(r, p, j, i, 0).start()

    def far_step(r, p, q):
        i, j = index(r, p, q), far_j(q)
        landed(block(r, p, j, core), t_in.at[r, p, j])

        @pl.when(jnp.logical_not(source))
        def _():
            outward(r, p, j, i, 0, pair).start()

        to_sibling(r, p, j, i, 1).start()

    def last_step(r, p, q):
        i, j = index(r, p, q), near_j(q)

        @pl.when(jnp.logical_not(source))
        def _():
            landed(block(r, p, j, core), t_in.at[r, p, j])
            to_sibling(r, p, j, i, 0).start()

    def own_rows(k):
        return 1, k // 2, 1 - k % 2

    def tokens_ready(r, p):
        for j in range(4):
            landed(block(r, p, j, 1 - core), t_sib.at[r, p, j])

    def partial(h, m):
        return remote(send.at[h, lines(m)], got.at[h, lines(m)], o_out.at[h, m], o_in.at[h, m], partner)

    def last_partial(g, m):
        h = last + g
        return remote(send.at[h, lines(m)], last_got.at[g, lines(m)], o_out.at[h, m], o_in.at[h, m], partner)

    def both(n):
        return jnp.concatenate([wb[2 * n], wb[2 * n + 1]], axis=1)

    def send_pair(n):
        weights_ready(2 * n)
        weights_ready(2 * n + 1)

        @pl.loop(0, PIECES)
        def _(m):
            part = jnp.dot(tokens_of(0, m), both(n), preferred_element_type=jnp.float32)
            for g in range(2):
                send[2 * n + g, lines(m), :] = encode(part[:, g * LANES : (g + 1) * LANES])
                partial(2 * n + g, m).start()

    def send_part(h):
        weights_ready(h)

        @pl.loop(0, PIECES)
        def _(m):
            part = jnp.dot(tokens_of(0, m), wb[h], preferred_element_type=jnp.float32)
            send[h, lines(m), :] = encode(part)

            @pl.when(h < last)
            def _():
                partial(h, m).start()

            @pl.when(h == last)
            def _():
                last_partial(0, m).start()

    def some(m, s):
        rows_of = jnp.concatenate([tb[0, m, s, c] for c in range(2)], axis=1)
        return jnp.dot(rows_of, wb[last + 1, pl.ds(pl.multiple_of(s * depth, depth), depth), :], preferred_element_type=jnp.float32)

    def last_up_ahead():
        landed(slot(last + 1, z_prev, depth // 2, depth // 2), w_in.at[last + 1, 2])
        landed(slot(last + 1, z_next, 0, depth // 2), w_in.at[last + 1, 3])

        @pl.loop(0, PIECES)
        def _(m):
            ahead[lines(m), :] = some(m, z) + some(m, z_prev) + some(m, z_next)

    def last_up():
        far = (z + 2) % 4
        landed(slot(last + 1, far, 0, depth // 2), w_in.at[last + 1, 4])
        landed(slot(last + 1, far, depth // 2, depth // 2), w_in.at[last + 1, 5])

        @pl.loop(0, PIECES)
        def _(m):
            send[last + 1, lines(m), :] = encode(ahead[lines(m), :] + some(m, far))
            last_partial(1, m).start()

    def last_own(g):
        @pl.loop(0, PIECES)
        def _(m):
            acc[lines(m), pl.ds(g * LANES, LANES)] = jnp.dot(tokens_of(1, m), wb[last + g], preferred_element_type=jnp.float32)
            kept_sums(g, m).start()

    def kept_sums(g, m):
        lane = pl.ds(g * LANES, LANES)
        return pltpu.make_async_copy(acc.at[lines(m), lane], last_own_sums.at[lines(m), lane], kept.at[g, m])

    def own_product(n, m):
        acc[lines(m), :] = jnp.dot(tokens_of(1, m), both(n), preferred_element_type=jnp.float32)

    def own_finish(n, m):
        landed(got.at[2 * n, lines(m)], o_in.at[2 * n, m])
        landed(got.at[2 * n + 1, lines(m)], o_in.at[2 * n + 1, m])

        @pl.loop(m * (piece // 32), (m + 1) * (piece // 32))
        def _(t):
            here = lines(t, 32)
            g = acc[here, :LANES] + decode(got[2 * n, here, :])
            u = acc[here, LANES:] + decode(got[2 * n + 1, here, :])
            out[n, here, :] = (g / (1.0 + jnp.exp(-g)) * u).astype(out.dtype)

        result(n, m).start()

    def result(n, m):
        lane = pl.ds(pl.multiple_of(n * LANES, LANES), LANES)
        return pltpu.make_async_copy(out.at[n, lines(m)], hidden.at[lines(m), lane], done.at[n, m])

    barrier = pltpu.get_barrier_semaphore()
    neighbours = (right, left, partner, flip, cross, sibling, pair, outer)
    for to in neighbours:
        pl.semaphore_signal(barrier, inc=1, device_id=to, device_id_type=MESH)
    for n in range(chunks):
        for copy in pack(n):
            copy.start()
    pl.semaphore_wait(barrier, len(neighbours))

    start_first(0)
    start_second(0)
    for p in range(PIECES):
        cross_step(p)

    @pl.when(source)
    def _():
        for p in range(PIECES):
            keep(p).start()

    start_first(1)

    early = (
        ((near_step, 0, 0, 0), (near_step, 0, 1, 0)),
        ((near_step, 0, 0, 1), (far_step, 0, 0, 0), (near_step, 0, 2, 0), (near_step, 0, 1, 1), (far_step, 0, 1, 0), (last_step, 0, 0, 0)),
        ((near_step, 0, 2, 1), (far_step, 0, 0, 1), (last_step, 0, 1, 0), (flip_step, 0)),
        ((near_step, *own_rows(0)), (far_step, 0, 2, 0), (last_step, 0, 0, 1), (flip_step, 1), (far_step, 0, 1, 1), (last_step, 0, 2, 0), (flip_step, 2)),
        ((near_step, *own_rows(1)), (near_step, *own_rows(2)), (far_step, 0, 2, 1), (last_step, 0, 1, 1)),
        ((last_step, 0, 2, 1), *((near_step, *own_rows(k)) for k in (3, 4, 5)), (far_step, *own_rows(0))),
    )
    for h, events in enumerate(early):
        weights_step(h)
        for event, *which in events:
            event(*which)
    for p in range(PIECES):
        tokens_ready(0, p)
    late = len(early)

    def unit(k):
        return jnp.where(k < 9, k % 3, 3 + (k - 9) // 3), jnp.where(k < 9, k // 3, (k - 9) % 3)

    def steps_at(h, counts):
        done = [jnp.int32(0)] + [jnp.int32(c) for c in counts]
        lo, hi = done[0], done[1]
        for i in range(1, len(counts)):
            lo = jnp.where(h >= late + i, done[i], lo)
            hi = jnp.where(h >= late + i, done[i + 1], hi)
        return lo, hi

    @pl.loop(late, last + 2)
    def _(h):
        weights_step(h)

        @pl.loop(*steps_at(h, (1, 3, 4, 5, 5, 5, 5, 5)))
        def _(k):
            far_step(*own_rows(k + 1))

        @pl.loop(*steps_at(h, (1, 2, 4, 5, 6, 6, 6, 6)))
        def _(k):
            last_step(*own_rows(k))

        @pl.loop(*steps_at(h, (2, 3, 4, 4, 5, 5, 5, 5)))
        def _(n):
            send_pair(n)

        @pl.loop(*steps_at(h, (10, 10, 10, 10, 10, 11, 12, 13)))
        def _(k):
            @pl.when(k >= 10)
            def _():
                send_part(k)

        @pl.when(jnp.logical_and(h >= 8, h <= 10))
        def _():
            tokens_ready(1, h - 8)

        @pl.loop(*steps_at(h, (0, 0, 2, 6, 10, 12, 18, 18)))
        def _(k):
            n, m = unit(k)
            own_product(n, m)

            @pl.when(k < 15)
            def _():
                own_finish(n, m)

    @pl.loop(0, PIECES)
    def _(m):
        own_finish(chunks - 2, m)

    last_up_ahead()
    last_up()
    last_own(0)
    last_own(1)

    @pl.loop(0, 2 * chunks)
    def _(h):
        for copy in first_half(h) + second_half(h) + relayed(h):
            copy.wait_send()

        @pl.when(h < last)
        def _():
            @pl.loop(0, PIECES)
            def _(m):
                partial(h, m).wait_send()

    @pl.loop(0, chunks - 1)
    def _(n):
        @pl.loop(0, PIECES)
        def _(m):
            result(n, m).wait()

    for p in range(PIECES):
        @pl.when(source)
        def _():
            flip_pass(p).wait_send()
            flip_send(p).wait_send()

    @pl.when(jnp.logical_not(source))
    def _():
        for p in range(PIECES):
            cross_send(p).wait_send()

    @pl.loop(0, steps)
    def _(i):
        r, p, j = i // (2 * PIECES), (i // 2) % PIECES, b * 2
        outward(r, p, j, i, 0, pair).wait_send()
        to_sibling(r, p, j, i, 0).wait_send()
        to_sibling(r, p, j, i, 1).wait_send()

        @pl.when(source)
        def _():
            outward(r, p, j, i, 1, outer).wait_send()

    for m in range(PIECES):
        for g in range(2):
            kept_sums(g, m).wait()
            last_partial(g, m).wait_send()
            landed(last_got.at[g, lines(m)], o_in.at[last + g, m])


def closing(hidden, last_own, last_got, out, whole, own, got, sem_in, sem_out):
    rows, units = out.shape
    piece = rows // PIECES
    known = units - LANES

    def lines(m):
        return pl.ds(m * piece, piece)

    def loads(m):
        return (
            pltpu.make_async_copy(last_own.at[lines(m)], own.at[lines(m)], sem_in.at[m, 0]),
            pltpu.make_async_copy(last_got.at[0, lines(m)], got.at[0, lines(m)], sem_in.at[m, 1]),
            pltpu.make_async_copy(last_got.at[1, lines(m)], got.at[1, lines(m)], sem_in.at[m, 2]),
            pltpu.make_async_copy(hidden.at[lines(m)], whole.at[lines(m), pl.ds(0, known)], sem_in.at[m, 3]),
        )

    def store(m):
        return pltpu.make_async_copy(whole.at[lines(m)], out.at[lines(m)], sem_out.at[m])

    for m in range(PIECES):
        for copy in loads(m):
            copy.start()
    for m in range(PIECES):
        for copy in loads(m):
            copy.wait()

        @pl.loop(m * (piece // 32), (m + 1) * (piece // 32))
        def _(t):
            here = pl.ds(pl.multiple_of(t * 32, 32), 32)
            g = own[here, :LANES] + decode(got[0, here, :])
            u = own[here, LANES:] + decode(got[1, here, :])
            whole[here, pl.ds(known, LANES)] = (g / (1.0 + jnp.exp(-g)) * u).astype(out.dtype)

        store(m).start()
    for m in range(PIECES):
        store(m).wait()


def on_device(tokens, gate_weight, up_weight):
    rows, half = tokens.shape
    depth, units = gate_weight.shape
    chunks = units // LANES
    dma = pltpu.SemaphoreType.DMA
    any_space = pl.BlockSpec(memory_space=pl.ANY)
    parts = pl.pallas_call(
        kernel,
        out_shape=(
            jax.ShapeDtypeStruct((rows, units - LANES), jnp.bfloat16),
            jax.ShapeDtypeStruct((rows, 2 * LANES), jnp.float32),
            jax.ShapeDtypeStruct((2, rows, LANES), jnp.bfloat16),
        ),
        in_specs=[any_space] * 3,
        out_specs=(any_space,) * 3,
        scratch_shapes=[
            pltpu.VMEM((2 * chunks, 4 * depth, LANES), jnp.bfloat16),
            pltpu.VMEM((2, PIECES, 4, 2, rows // PIECES, half), jnp.bfloat16),
            pltpu.VMEM((2 * chunks, rows, LANES), jnp.bfloat16),
            pltpu.VMEM((2 * chunks, rows, LANES), jnp.bfloat16),
            pltpu.VMEM((rows, 2 * LANES), jnp.float32),
            pltpu.VMEM((rows, LANES), jnp.float32),
            pltpu.VMEM((chunks, rows, LANES), jnp.bfloat16),
            dma((2 * chunks, 6)),
            dma((2 * chunks, 6)),
            dma((2 * chunks,)),
            dma((2, PIECES, 4)),
            dma((2, PIECES, 4)),
            dma((2, PIECES)),
            dma((4 * PIECES, 2)),
            dma((4 * PIECES, 2)),
            dma((2 * chunks, PIECES)),
            dma((2 * chunks, PIECES)),
            dma((chunks, PIECES)),
            dma((2, PIECES)),
        ],
        compiler_params=pltpu.CompilerParams(
            collective_id=0, has_side_effects=True, vmem_limit_bytes=60 * 2**20
        ),
        cost_estimate=pl.CostEstimate(
            flops=2 * rows * 16 * half * units * 2, bytes_accessed=2 * (rows * half + 2 * depth * units + rows * units), transcendentals=0
        ),
    )(tokens, gate_weight, up_weight)
    return pl.pallas_call(
        closing,
        out_shape=jax.ShapeDtypeStruct((rows, units), jnp.bfloat16),
        in_specs=[any_space] * 3,
        out_specs=any_space,
        scratch_shapes=[
            pltpu.VMEM((rows, units), jnp.bfloat16),
            pltpu.VMEM((rows, 2 * LANES), jnp.float32),
            pltpu.VMEM((2, rows, LANES), jnp.bfloat16),
            dma((PIECES, 4)),
            dma((PIECES,)),
        ],
    )(*parts)


def solution(mesh):
    placed = (P("row", "col"), P("row", "col"), P("row", "col"))
    return jax.shard_map(
        on_device, mesh=mesh, in_specs=placed, out_specs=P("row", "col"), check_vma=False
    )
```
